512 devices in a mesh: dp: 32 (over x, z), seq: 16 (over y, core).
Axes of the slice: x: 4, y: 8, z: 8, core: 2. Of those that a mesh axis runs over, the one named last changes fastest.
Arguments:
- projected: bfloat16 [32, 2048, 3, 1536], P('dp', 'seq'), may hold values from -6 to 6
- cotangent: bfloat16 [32, 2048, 1152], P('dp', 'seq'), may hold values from -6 to 6
- out_weight: bfloat16 [1536, 1152], P('seq'), may hold values from -0.15625 to 0.15625
- norm_gain: float32 [1536], replicated, may hold values from 0.1 to 1.9
- conv_taps: float32 [9, 1536], replicated, may hold values from -2.5 to 2.5
- feature_seeds: int32 [48], replicated, may hold values from 0 to 1073741823
- packing: int32 [32, 5, 2048], P('dp', None, 'seq'), may hold values from 0 to 68, as said below
Outputs:
- block_out: bfloat16 [32, 2048, 1152], P('dp', 'seq')
- grad_projected: bfloat16 [32, 2048, 3, 1536], P('dp', 'seq')
- grad_out_weight: float32 [1536, 1152], P('seq')
- grad_norm_gain: float32 [1536], replicated
- grad_conv_taps: float32 [9, 1536], replicated
The draws below stay inside these ranges and needn't reach their ends.
Inputs may be any that keep to these rules, and one draw needn't show every extreme that they name: `packing`: in each pack, images 0 to 2 follow one another, each contiguous and row-major; rows 1 and 2 give a token's row and column in its image, rows 3 and 4 the image's width and height. Widths are multiples of 16 up to 64; image 1 of every pack is 64 wide and directly precedes the last image; the last image of every pack is 16 wide and holds the pack's last 1088 tokens; heights are at least 2; every pack holds 3 images and no padding.
All inputs are finite; a program needn't handle non-finite values.
Results may differ from the reference program's by a relative error of at most 0.012.
Values may be sent and summed in bfloat16 or wider, within the bound.
No kernel may reach another device: no remote copies, remote signals or barrier semaphores. Data moves between devices by JAX's collectives and lax.ppermute only.
A program may use at most 128 MiB of HBM per device.

```python
import math
import jax
import jax.numpy as jnp
from jax import lax

D = 1152
HEAD = 32
FEAT = 256
HEADS = 48
A = 1536
TOK_DEV = 128
TOKENS = 2048
PACKS = 32
IMGS = 3
WMAX = 64
UNIT = 16
HMAX = 8


def one_packing(pack_key):
    key_width, key_height = jax.random.split(pack_key)
    width_steps = WMAX // UNIT
    last_tokens = TOKENS // 2 + TOK_DEV - WMAX
    front_tokens = TOKENS - last_tokens
    widths_mid = UNIT * jax.random.randint(key_width, (IMGS - 2,), 1, width_steps + 1, dtype=jnp.int32)
    widths_mid = widths_mid.at[IMGS - 3].set(WMAX)
    heights_mid = jax.random.randint(key_height, (IMGS - 2,), 2, HMAX + 1, dtype=jnp.int32)
    remain = front_tokens - jnp.sum(widths_mid * heights_mid)
    quotient = remain // UNIT
    factors = jnp.arange(1, width_steps + 1, dtype=jnp.int32)
    usable = (quotient % factors == 0) & (quotient >= 2 * factors)
    fitting = jnp.max(jnp.where(usable, factors, 1))
    width_first = UNIT * fitting
    height_first = remain // width_first
    width_last = jnp.full((1,), UNIT, jnp.int32)
    height_last = jnp.full((1,), last_tokens // UNIT, jnp.int32)
    widths = jnp.concatenate([width_first[None], widths_mid, width_last]).astype(jnp.int32)
    heights = jnp.concatenate([height_first[None], heights_mid, height_last]).astype(jnp.int32)
    image_sizes = widths * heights
    starts = jnp.cumsum(image_sizes) - image_sizes
    position = jnp.arange(TOKENS, dtype=jnp.int32)
    image_of = jnp.sum((position[:, None] >= starts[None, 1:]).astype(jnp.int32), axis=1).astype(jnp.int32)
    offset = position - starts[image_of]
    width_of = widths[image_of]
    height_of = heights[image_of]
    return jnp.stack([image_of, offset // width_of, offset % width_of, width_of, height_of]).astype(jnp.int32)


def draw_packing(key, part):
    pack_keys = jax.random.split(jax.random.fold_in(key, 7), PACKS)
    return jax.vmap(one_packing)(pack_keys)


def touch_ends(values, key, least, largest):
    longest = values.shape.index(max(values.shape))
    spots = []
    for shift in (0, 1):
        where = [jax.random.randint(jax.random.fold_in(key, axis), (), 0, length) for axis, length in enumerate(values.shape)]
        where[longest] = (where[longest] + shift) % values.shape[longest]
        spots.append(tuple(where))
    return values.at[spots[0]].set(least).at[spots[1]].set(largest)


def block_scale(key, shape, shards, smallest, top_value):
    def one(dim, parts):
        draws = jax.random.uniform(jax.random.fold_in(jax.random.fold_in(key, 6), dim), (parts,), jnp.float32, smallest / len(shards), top_value / len(shards))
        return jnp.repeat(jnp.exp(draws), shape[dim] // parts).reshape((-1,) + (1,) * (len(shape) - dim - 1))

    level = one(*shards[0])
    for cut in shards[1:]:
        level = level * one(*cut)
    return level


def scatter_about(key, shape, scale, most, cuts=(), kind=jnp.bfloat16):
    entries = jax.random.normal(key, shape, jnp.float32) * scale
    if len(cuts) > 0:
        entries = block_scale(key, shape, cuts, -0.22, 0.18) * entries
    return jnp.clip(entries, min=-most, max=most).astype(kind)


def setup_inputs(seed: int = 0) -> dict:
    arg_keys = jax.random.split(jax.random.key(seed), 8)
    projected = scatter_about(arg_keys[0], (PACKS, TOKENS, 3, A), 1.0, 6.0, ((0, 32), (1, 16)))
    cotangent = scatter_about(arg_keys[1], (PACKS, TOKENS, D), 1.0, 6.0, ((0, 32), (1, 16)))
    out_weight = scatter_about(arg_keys[2], (A, D), A ** -0.5, 0.15625, ((0, 16),))
    norm_gain = jnp.clip(1.0 + 0.18 * jax.random.normal(arg_keys[3], (A,), jnp.float32), 0.1, 1.9)
    conv_taps = scatter_about(arg_keys[4], (9, A), 0.4, 2.5, (), jnp.float32)
    feature_seeds = touch_ends(jax.random.randint(arg_keys[5], (HEADS,), 0, 1073741824), jax.random.fold_in(arg_keys[5], 1), 0, 1073741823).astype(jnp.int32)
    packing = draw_packing(jax.random.fold_in(arg_keys[7], 71), 0)
    return {"projected": projected, "cotangent": cotangent, "out_weight": out_weight, "norm_gain": norm_gain, "conv_taps": conv_taps, "feature_seeds": feature_seeds, "packing": packing}


feature_floor = 0.1
epsilon = 1e-06
highest = lax.Precision.HIGHEST

def feature_matrix(seed_list):
    counter = jnp.arange(HEAD * FEAT, dtype=jnp.int32).reshape(1, HEAD, FEAT)
    hashed = seed_list.astype(jnp.int32)[:, None, None] * -1640531535 + counter
    hashed = hashed ^ hashed >> 16 & 65535
    hashed = hashed * -2048144789
    hashed = hashed ^ hashed >> 13 & 524287
    hashed = hashed * -1028477387
    hashed = hashed ^ hashed >> 16 & 65535
    top_bits = hashed >> 8 & 16777215
    uniform = top_bits.astype(jnp.float32) * (1.0 / 16777216.0)
    return (1.7320508 * (2.0 * uniform - 1.0)).astype(jnp.bfloat16)

def neighbour(values, packing_rows, tap_index, direction):
    row_count = values.shape[0]
    step_row = tap_index // 3 - 1
    step_col = tap_index % 3 - 1
    position = jnp.arange(row_count, dtype=jnp.int32)
    row_width = packing_rows[3]
    new_row = packing_rows[1] + direction * step_row
    new_col = packing_rows[2] + direction * step_col
    inside = (new_row >= 0) & (new_row < packing_rows[4]) & (new_col >= 0) & (new_col < row_width)
    source = jnp.clip(position + direction * (step_row * row_width + step_col), 0, row_count - 1).astype(jnp.int32)
    return jnp.where(inside[:, None], values[source], jnp.zeros((), values.dtype))

def depthwise(values, packing_rows, tap_table, direction):
    running = jnp.zeros(values.shape, jnp.float32)
    for tap_index in range(9):
        running = running + tap_table[tap_index][None, :] * neighbour(values, packing_rows, tap_index, direction).astype(jnp.float32)
    return running

def tap_grads(grad_conv, values, packing_rows):
    grad_float = grad_conv.astype(jnp.float32)
    return jnp.stack([lax.optimization_barrier(jnp.sum(grad_float * neighbour(values, packing_rows, tap_index, 1).astype(jnp.float32), axis=0)) for tap_index in range(9)])

def reference(projected, cotangent, out_weight, norm_gain, conv_taps, feature_seeds, packing):
    width_all = out_weight.shape[0]
    head_count = width_all // HEAD
    omegas = feature_matrix(feature_seeds).astype(jnp.float32)
    feature_scale = 1.0 / math.sqrt(HEAD)

    def one_pack(running, inputs):
        grad_weight, grad_gain, grad_taps = running
        tokens_in, grad_in, rows_in = inputs
        tok_rows = tokens_in.shape[0]
        conv_values = depthwise(tokens_in[:, 2], rows_in, conv_taps, 1).astype(jnp.bfloat16)
        queries = tokens_in[:, 0].reshape(tok_rows, head_count, HEAD).astype(jnp.float32)
        keys_in = tokens_in[:, 1].reshape(tok_rows, head_count, HEAD).astype(jnp.float32)
        values_c = conv_values.reshape(tok_rows, head_count, HEAD).astype(jnp.float32)
        onehot = (rows_in[0][:, None] == jnp.arange(IMGS, dtype=jnp.int32)[None, :]).astype(jnp.float32)
        pre_query = jnp.einsum('the,hef->thf', queries, omegas, precision=highest) * feature_scale
        pre_key = jnp.einsum('the,hef->thf', keys_in, omegas, precision=highest) * feature_scale
        feat_query = (jax.nn.relu(pre_query) + feature_floor).astype(jnp.bfloat16).astype(jnp.float32)
        feat_key = (jax.nn.relu(pre_key) + feature_floor).astype(jnp.bfloat16).astype(jnp.float32)
        masked_values = onehot[:, :, None, None] * values_c[:, None]
        states = jnp.einsum('thf,tihe->hife', feat_key, masked_values, precision=highest).astype(jnp.bfloat16).astype(jnp.float32)
        totals = jnp.einsum('thf,ti->hif', feat_key, onehot, precision=highest).astype(jnp.bfloat16).astype(jnp.float32)
        numerator = lax.optimization_barrier(jnp.sum(jnp.einsum('thf,hife->thie', feat_query, states, precision=highest) * onehot[:, None, :, None], axis=2))
        denominator = lax.optimization_barrier(jnp.sum(jnp.einsum('thf,hif->thi', feat_query, totals, precision=highest) * onehot[:, None, :], axis=2))
        attention = (numerator / denominator[..., None]).astype(jnp.bfloat16).reshape(tok_rows, width_all)
        attn_float = attention.astype(jnp.float32)
        inv_rms = lax.rsqrt(lax.optimization_barrier(jnp.mean(attn_float * attn_float, axis=1)) + epsilon)
        normed = (attn_float * norm_gain[None, :] * inv_rms[:, None]).astype(jnp.bfloat16)
        block_out = jnp.dot(normed, out_weight, preferred_element_type=jnp.float32).astype(jnp.bfloat16)
        grad_normed = jnp.dot(grad_in, out_weight.T, preferred_element_type=jnp.float32)
        pack_gain = lax.optimization_barrier(jnp.sum(grad_normed * attn_float * inv_rms[:, None], axis=0))
        inner_sum = lax.optimization_barrier(jnp.sum(norm_gain[None, :] * grad_normed * attn_float, axis=1))
        grad_attention = (inv_rms[:, None] * norm_gain[None, :] * grad_normed - attn_float * (inv_rms ** 3 * inner_sum / width_all)[:, None]).astype(jnp.bfloat16)
        pack_weight = jnp.dot(normed.T, grad_in, preferred_element_type=jnp.float32)
        grad_heads = grad_attention.reshape(tok_rows, head_count, HEAD).astype(jnp.float32)
        grad_numer = (grad_heads / denominator[..., None]).astype(jnp.bfloat16).astype(jnp.float32)
        grad_denom = -lax.optimization_barrier(jnp.sum(grad_heads * numerator, axis=-1)) / (denominator * denominator)
        masked_grad = onehot[:, :, None, None] * grad_numer[:, None]
        weighted = onehot[:, :, None] * grad_denom[:, None, :]
        grad_states = jnp.einsum('thf,tihe->hife', feat_query, masked_grad, precision=highest).astype(jnp.bfloat16).astype(jnp.float32)
        grad_totals = jnp.einsum('thf,tih->hif', feat_query, weighted, precision=highest).astype(jnp.bfloat16).astype(jnp.float32)
        grad_fq = jnp.einsum('tihe,hife->thf', masked_grad, states, precision=highest) + jnp.einsum('tih,hif->thf', weighted, totals, precision=highest)
        gate_query = jnp.where(pre_query > 0, grad_fq, 0.0).astype(jnp.bfloat16).astype(jnp.float32)
        grad_queries = (jnp.einsum('thf,hef->the', gate_query, omegas, precision=highest) * feature_scale).astype(jnp.bfloat16)
        grad_fk = jnp.einsum('tihe,hife->thf', masked_values, grad_states, precision=highest) + jnp.einsum('ti,hif->thf', onehot, grad_totals, precision=highest)
        gate_key = jnp.where(pre_key > 0, grad_fk, 0.0).astype(jnp.bfloat16).astype(jnp.float32)
        grad_keys = (jnp.einsum('thf,hef->the', gate_key, omegas, precision=highest) * feature_scale).astype(jnp.bfloat16)
        grad_conv = lax.optimization_barrier(jnp.sum(jnp.einsum('thf,hife->thie', feat_key, grad_states, precision=highest) * onehot[:, None, :, None], axis=2))
        grad_conv = grad_conv.astype(jnp.bfloat16).reshape(tok_rows, width_all)
        grad_values = depthwise(grad_conv, rows_in, conv_taps, -1).astype(jnp.bfloat16)
        pack_taps = tap_grads(grad_conv, tokens_in[:, 2], rows_in)
        grad_tokens = jnp.stack([grad_queries.reshape(tok_rows, width_all), grad_keys.reshape(tok_rows, width_all), grad_values], axis=1)
        return ((grad_weight + pack_weight, grad_gain + pack_gain, grad_taps + pack_taps), (block_out, grad_tokens))
    start_sums = (jnp.zeros(out_weight.shape, jnp.float32), jnp.zeros((width_all,), jnp.float32), jnp.zeros((9, width_all), jnp.float32))
    sums, stacked = lax.scan(one_pack, start_sums, (projected, cotangent, packing))
    pack_count = projected.shape[0]
    return (stacked[0], stacked[1], sums[0] / pack_count, sums[1] / pack_count, sums[2] / pack_count)
```

```python
import math

import jax
import jax.numpy as jnp
from jax import lax
from jax.experimental import pallas as pl
from jax.experimental.pallas import tpu as pltpu
from jax.sharding import PartitionSpec as P

HEAD = 32
FEAT = 256
LANES = 128
CHUNK = 256
WIDTHS = (16, 32, 48, 64)

feature_floor = 0.1
epsilon = 1e-06
scale = 1.0 / math.sqrt(HEAD)
bf16, f32 = jnp.bfloat16, jnp.float32


def dot(a, b):
    return lax.dot_general(a, b, (((1,), (0,)), ((), ())), preferred_element_type=f32)


def dot_nt(a, b):
    return lax.dot_general(a, b, (((1,), (1,)), ((), ())), preferred_element_type=f32)


def omega_of(seed, e, f):
    hashed = seed * -1640531535 + (e * FEAT + f)
    hashed = hashed ^ ((hashed >> 16) & 65535)
    hashed = hashed * -2048144789
    hashed = hashed ^ ((hashed >> 13) & 524287)
    hashed = hashed * -1028477387
    hashed = hashed ^ ((hashed >> 16) & 65535)
    uniform = ((hashed >> 8) & 16777215).astype(f32) * (1.0 / 16777216.0)
    return 1.7320508 * (2.0 * uniform - 1.0)


def omega_tall(seed_row, heads):
    shape = (FEAT, heads * HEAD)
    lane = lax.broadcasted_iota(jnp.int32, shape, 1)
    block = omega_of(seed_row, lane % HEAD, lax.broadcasted_iota(jnp.int32, shape, 0))
    return jnp.concatenate(
        [jnp.where(lane // HEAD == h, block, 0.0) for h in range(heads)], axis=0
    ).astype(bf16)


def omega_wide(seed_column, heads):
    shape = (heads * HEAD, FEAT)
    row = lax.broadcasted_iota(jnp.int32, shape, 0)
    block = omega_of(seed_column, row % HEAD, lax.broadcasted_iota(jnp.int32, shape, 1))
    return jnp.concatenate(
        [jnp.where(row // HEAD == h, block, 0.0) for h in range(heads)], axis=1
    ).astype(bf16)


def head_mask(heads):
    shape = (LANES, heads * FEAT)
    row = lax.broadcasted_iota(jnp.int32, shape, 0)
    column = lax.broadcasted_iota(jnp.int32, shape, 1) // FEAT
    width = heads * HEAD
    channel = (row < width) & (row // HEAD == column)
    total = (row >= width) & (row < width + 3 * heads) & ((row - width) % heads == column)
    return channel | total


def chunk_of(ref, part, width, j):
    rows = pl.ds(part * width, width)
    return jnp.concatenate([ref[2 * j, rows, :], ref[2 * j + 1, rows, :]], axis=1)


def part_of(ref, start, count):
    return jnp.concatenate(
        [ref[s, pl.ds(start, count), :] for s in range(ref.shape[0])], axis=1
    )


def by_head(rows, heads):
    return jnp.concatenate(
        [jnp.broadcast_to(rows[h : h + 1], (HEAD, rows.shape[1])) for h in range(heads)], axis=0
    )


def head_sums(values, heads):
    return [
        jnp.sum(values[h * HEAD : (h + 1) * HEAD], axis=0, keepdims=True) for h in range(heads)
    ]


def shifted(values, shift):
    return pltpu.roll(values, shift % values.shape[1], axis=1)


class Grid:
    def __init__(self, ref, start):
        packing = part_of(ref, start, 16).astype(f32)
        self.image, self.row, self.column, self.width, self.height = (
            packing[i : i + 1] for i in range(5)
        )
        self.left = self.column > 0.5
        self.right = self.column < self.width - 1.5
        self.above = self.row > 0.5
        self.below = self.row < self.height - 1.5

    def column_before(self, values):
        return jnp.where(self.left, shifted(values, 1), 0.0)

    def column_after(self, values):
        return jnp.where(self.right, shifted(values, -1), 0.0)

    def by_rows(self, values, inside, sign):
        half = values.shape[1] // 2
        moved = jnp.where(inside & (self.width == 16.0), shifted(values, sign * 16), 0.0)
        front, back = moved[:, :half], moved[:, half:]
        for width in WIDTHS[1:]:
            mask = inside[:, :half] & (self.width[:, :half] == float(width))
            front = front + jnp.where(mask, shifted(values[:, :half], sign * width), 0.0)
        return jnp.concatenate([front, back], axis=1)

    def row_above(self, values):
        return self.by_rows(values, self.above, 1)

    def row_below(self, values):
        return self.by_rows(values, self.below, -1)


def features(pre):
    return (jnp.maximum(pre, 0.0) + feature_floor).astype(bf16)


def split_images(rows, image, j, middle):
    zero = jnp.zeros((), rows.dtype)
    front = back = None
    if j < middle:
        front = jnp.concatenate(
            [jnp.where(image == 0.0, rows, zero), jnp.where(image == 1.0, rows, zero)], axis=0
        ).astype(bf16)
    if j >= middle - 1:
        back = jnp.where(image == 2.0, rows, zero).astype(bf16)
    return front, back


def add(total, term):
    return term if total is None else total + term


def pick_image(left, right, image, j, middle, rows):
    if j < middle - 1:
        both = dot(left[: 2 * LANES], right)
        return jnp.where(image == 0.0, both[:rows], both[LANES : LANES + rows])
    if j >= middle:
        return dot(left[2 * LANES :], right)[:rows]
    every = dot(left, right)
    front = jnp.where(image == 0.0, every[:rows], every[LANES : LANES + rows])
    return jnp.where(image == 2.0, every[2 * LANES : 2 * LANES + rows], front)


def ones_rows(width, columns, count):
    row = lax.broadcasted_iota(jnp.int32, (LANES - width, columns), 0)
    return jnp.where(row < count, 1.0, 0.0)


def forward_kernel(heads, x_ref, taps_ref, seed_row_ref, weight_ref,
                   numer_ref, denom_ref, states_ref, conv_ref, weight_out):
    width = heads * HEAD
    chunks = x_ref.shape[0] * LANES // CHUNK
    middle = chunks // 2
    weight_out[...] = weight_ref[...]
    grid = Grid(x_ref, 3 * width)
    values = part_of(x_ref, 2 * width, width).astype(f32)
    taps = taps_ref[...]
    trio = (grid.column_before(values), values, grid.column_after(values))

    def row_of_taps(r):
        return sum(taps[:, 3 * r + c : 3 * r + c + 1] * trio[c] for c in range(3))

    conv = row_of_taps(1) + grid.row_above(row_of_taps(0)) + grid.row_below(row_of_taps(2))
    conv_ref[...] = conv.astype(bf16)
    omega = omega_tall(seed_row_ref[...], heads)
    front = back = None
    for j in range(chunks):
        lanes = pl.ds(j * CHUNK, CHUNK)
        image = grid.image[:, j * CHUNK : (j + 1) * CHUNK]
        rows = jnp.concatenate(
            [conv_ref[:, lanes].astype(f32), ones_rows(width, CHUNK, 3 * heads)], axis=0
        )
        feat_key = features(dot(omega, chunk_of(x_ref, 1, width, j)) * scale)
        first, last = split_images(rows, image, j, middle)
        if first is not None:
            front = add(front, dot_nt(first, feat_key))
        if last is not None:
            back = add(back, dot_nt(last, feat_key))
    mask = head_mask(heads)
    states = jnp.concatenate(
        [
            jnp.where(mask, part, 0.0).astype(bf16)
            for part in (front[:LANES], front[LANES:], back)
        ],
        axis=0,
    )
    states_ref[...] = states
    for j in range(chunks):
        lanes = pl.ds(j * CHUNK, CHUNK)
        image = grid.image[:, j * CHUNK : (j + 1) * CHUNK]
        feat_query = features(dot(omega, chunk_of(x_ref, 0, width, j)) * scale)
        both = pick_image(states, feat_query, image, j, middle, width + 8)
        numer_ref[:, lanes] = both[:width]
        denom_ref[:, lanes] = both[width : width + 8]


def sums_kernel(heads, numer_ref, denom_ref, weight_ref, cotangent_ref, gain_ref,
                grad_normed_ref, sums_ref):
    chunks = numer_ref.shape[1] // CHUNK
    weight, gain = weight_ref[...], gain_ref[...]
    squares, inner = [], []
    for j in range(chunks):
        lanes = pl.ds(j * CHUNK, CHUNK)
        grad_normed = dot_nt(weight, cotangent_ref[pl.ds(j * CHUNK, CHUNK), :])
        grad_normed_ref[:, lanes] = grad_normed
        attention = (numer_ref[:, lanes] / by_head(denom_ref[:, lanes], heads)).astype(bf16)
        attention = attention.astype(f32)
        square = jnp.sum(attention * attention, axis=0, keepdims=True)
        product = jnp.sum(gain * grad_normed * attention, axis=0, keepdims=True)
        for part in range(CHUNK // LANES):
            here = slice(part * LANES, (part + 1) * LANES)
            squares.append(square[:, here])
            inner.append(product[:, here])
    both = jnp.concatenate(squares + inner, axis=0)
    for peer in range(sums_ref.shape[0]):
        sums_ref[peer] = both


def normed_kernel(heads, numer_ref, denom_ref, grad_normed_ref, sums_ref, gain_ref, cotangent_ref,
                  normed_ref, grad_ref, weight_ref, gain_out):
    chunks = numer_ref.shape[1] // CHUNK
    groups = sums_ref.shape[0]
    width = heads * HEAD
    gain = gain_ref[...]
    sums = jnp.sum(sums_ref[...], axis=0)
    inverse = lax.rsqrt(sums[:groups] * (1.0 / (width * groups)) + epsilon)
    inner = inverse * inverse * inverse * sums[groups:] * (1.0 / (width * groups))
    weight = gain_sum = None
    for j in range(chunks):
        lanes = pl.ds(j * CHUNK, CHUNK)

        def tokens(values):
            return jnp.concatenate([values[2 * j : 2 * j + 1], values[2 * j + 1 : 2 * j + 2]], axis=1)

        inv_rms, away = tokens(inverse), tokens(inner)
        grad_normed = grad_normed_ref[:, lanes]
        attention = (numer_ref[:, lanes] / by_head(denom_ref[:, lanes], heads)).astype(bf16)
        attention = attention.astype(f32)
        normed = (attention * gain * inv_rms).astype(bf16)
        grad_ref[:, lanes] = inv_rms * gain * grad_normed - attention * away
        gain_sum = add(gain_sum, grad_normed * attention * inv_rms)
        for part in range(CHUNK // LANES):
            normed_ref[2 * j + part] = normed[:, part * LANES : (part + 1) * LANES]
        weight = add(weight, dot(normed, cotangent_ref[pl.ds(j * CHUNK, CHUNK), :]))
    gain_out[...] = jnp.broadcast_to(jnp.sum(gain_sum, axis=1, keepdims=True), gain_out.shape)
    across = weight.shape[1] // LANES
    for r in range(width // 8):
        for c in range(across):
            weight_ref[pl.ds((r * across + c) * 8, 8), :] = weight[
                r * 8 : (r + 1) * 8, c * LANES : (c + 1) * LANES
            ]
    used = width * across
    weight_ref[used:, :] = jnp.zeros((weight_ref.shape[0] - used, LANES), f32)


def backward_kernel(heads, x_ref, taps_ref, seed_row_ref, seed_column_ref, numer_ref, denom_ref,
                    states_ref, conv_ref, normed_ref, grad_ref, gain_ref,
                    out_ref, small_ref, grad_conv_ref):
    width = heads * HEAD
    chunks = x_ref.shape[0] * LANES // CHUNK
    middle = chunks // 2
    grid = Grid(x_ref, 3 * width)
    omega = omega_tall(seed_row_ref[...], heads)
    omega_back = omega_wide(seed_column_ref[...], heads)
    states = jnp.transpose(states_ref[...].astype(f32)).astype(bf16)
    mask = head_mask(heads)
    front = back = None

    def put(part, j, values):
        for half in range(CHUNK // LANES):
            out_ref[2 * j + half, pl.ds(part * width, width), :] = values[
                :, half * LANES : (half + 1) * LANES
            ]

    def spread(table, first, last):
        total = None
        if first is not None:
            total = add(total, dot(table[:, : 2 * LANES], first))
        if last is not None:
            total = add(total, dot(table[:, 2 * LANES :], last))
        return total

    for j in range(chunks):
        lanes = pl.ds(j * CHUNK, CHUNK)
        image = grid.image[:, j * CHUNK : (j + 1) * CHUNK]
        pre = dot(omega, chunk_of(x_ref, 0, width, j)) * scale
        feat_query = features(pre)
        grad = grad_ref[:, lanes].astype(bf16).astype(f32)
        denom = denom_ref[:, lanes]
        grad_numer = (grad / by_head(denom, heads)).astype(bf16).astype(f32)
        dots = head_sums(grad * numer_ref[:, lanes], heads)
        row = lax.broadcasted_iota(jnp.int32, (LANES - width, CHUNK), 0)
        extra = jnp.zeros((LANES - width, CHUNK), f32)
        for h in range(heads):
            below = denom[h : h + 1]
            rest = -dots[h] / (below * below)
            for level in range(3):
                high = rest.astype(bf16).astype(f32)
                extra = jnp.where(row == level * heads + h, high, extra)
                rest = rest - high
        rows = jnp.concatenate([grad_numer, extra], axis=0)
        first, last = split_images(rows, image, j, middle)
        if first is not None:
            front = add(front, dot_nt(first, feat_query))
        if last is not None:
            back = add(back, dot_nt(last, feat_query))
        gate = jnp.where(pre > 0, spread(states, first, last), 0.0).astype(bf16)
        put(1, j, (dot(omega_back, gate) * scale).astype(bf16))
    parts = []
    for part in (front[:LANES], front[LANES:], back):
        part = jnp.where(mask, part, 0.0)
        total = jnp.sum(part[width:], axis=0, keepdims=True)
        row = lax.broadcasted_iota(jnp.int32, (LANES - width, heads * FEAT), 0)
        parts.append(part[:width])
        parts.append(jnp.where(row == 0, total, 0.0))
    grad_states = jnp.concatenate(parts, axis=0)
    table = jnp.transpose(grad_states).astype(bf16)
    grad_states = grad_states.astype(bf16)
    for j in range(chunks):
        lanes = pl.ds(j * CHUNK, CHUNK)
        image = grid.image[:, j * CHUNK : (j + 1) * CHUNK]
        pre = dot(omega, chunk_of(x_ref, 1, width, j)) * scale
        feat_key = features(pre)
        rows = jnp.concatenate(
            [conv_ref[:, lanes].astype(f32), ones_rows(width, CHUNK, 1)], axis=0
        )
        first, last = split_images(rows, image, j, middle)
        gate = jnp.where(pre > 0, spread(table, first, last), 0.0).astype(bf16)
        put(2, j, (dot(omega_back, gate) * scale).astype(bf16))
        grad_conv_ref[:, lanes] = (
            pick_image(grad_states, feat_key, image, j, middle, width).astype(bf16).astype(f32)
        )
    grad_conv = grad_conv_ref[...]
    values = part_of(x_ref, 2 * width, width).astype(f32)
    taps = taps_ref[...]
    trio = (grid.column_before(values), values, grid.column_after(values))
    moved = (grid.row_below(grad_conv), grad_conv, grid.row_above(grad_conv))
    lane = lax.broadcasted_iota(jnp.int32, (width, LANES), 1)
    small = jnp.where(lane == 9, gain_ref[...], 0.0)
    for r in range(3):
        for c in range(3):
            total = jnp.sum(moved[r] * trio[c], axis=1, keepdims=True)
            small = jnp.where(lane == 3 * r + c, total, small)

    def column_of_taps(c):
        return sum(taps[:, 3 * r + c : 3 * r + c + 1] * moved[r] for r in range(3))

    grad_values = (
        column_of_taps(1)
        + grid.column_after(column_of_taps(0))
        + grid.column_before(column_of_taps(2))
    ).astype(bf16)
    small = jnp.concatenate([small, jnp.zeros((LANES - width, LANES), f32)], axis=0)
    small_ref[...] = jnp.transpose(small)[: small_ref.shape[0]]
    for s in range(x_ref.shape[0]):
        out_ref[s, pl.ds(0, width), :] = normed_ref[s]
        out_ref[s, pl.ds(3 * width, width), :] = grad_values[:, s * LANES : (s + 1) * LANES]
        out_ref[s, pl.ds(4 * width, 16), :] = jnp.zeros((16, LANES), bf16)


def pack_sum_kernel(parts_ref, small_ref, out_ref):
    packs = parts_ref.shape[0]
    rows = parts_ref.shape[1]
    total = jnp.sum(parts_ref[...], axis=0) * (1.0 / packs)
    small = small_ref[...]
    for peer in range(packs):
        out_ref[peer, pl.ds(0, rows), :] = total
        out_ref[peer, pl.ds(rows, 16), :] = small


def unpack_kernel(gathered_ref, outgoing_ref, weight_ref, payload_ref):
    packs = gathered_ref.shape[0]
    rows = gathered_ref.shape[1] - 16
    width, features_out = weight_ref.shape
    across = features_out // LANES
    for r in range(width // 8):
        for c in range(across):
            start = (r * across + c) * 8
            weight_ref[pl.ds(r * 8, 8), pl.ds(c * LANES, LANES)] = gathered_ref[
                start // rows, pl.ds(start % rows, 8), :
            ]
    small = jnp.sum(gathered_ref[:, pl.ds(rows, 16), :], axis=0) * (1.0 / packs)
    for peer in range(payload_ref.shape[0]):
        payload_ref[peer] = small.astype(bf16)


def call(kernel, name, out_shapes, operands, scratch=(), **more):
    return pl.pallas_call(
        kernel,
        name=name,
        out_shape=[jax.ShapeDtypeStruct(shape, kind) for shape, kind in out_shapes],
        scratch_shapes=list(scratch),
        compiler_params=pltpu.CompilerParams(vmem_limit_bytes=56 * 1024 * 1024),
        **more,
    )(*operands)


def swap(blocks, axis):
    return lax.all_to_all(blocks, axis, split_axis=0, concat_axis=0, tiled=True)


def local(projected, cotangent, out_weight, norm_gain, conv_taps, feature_seeds, packing):
    groups = lax.axis_size("seq")
    member = lax.axis_index("seq")
    packs = lax.axis_size("dp")
    tokens, _, width_all = projected.shape[1:]
    features_out = cotangent.shape[2]
    width = width_all // groups
    heads = width // HEAD
    all_tokens = tokens * groups
    cotangent_all = lax.all_gather(cotangent[0], "seq", axis=0, tiled=True)
    by_peer = projected[0].transpose(1, 2, 0).reshape(3, groups, width, tokens)
    by_peer = by_peer.transpose(1, 0, 2, 3).reshape(groups, 3 * width, tokens)
    rows = jnp.pad(packing[0].astype(bf16), ((0, 11), (0, 0)))
    outgoing = jnp.concatenate(
        [by_peer, jnp.broadcast_to(rows[None], (groups, 16, tokens))], axis=1
    )
    seeds = jnp.repeat(lax.dynamic_slice_in_dim(feature_seeds, member * heads, heads, 0), HEAD)
    taps = jnp.pad(
        lax.dynamic_slice_in_dim(conv_taps, member * width, width, 1).T, ((0, 0), (0, 7))
    )
    gain = lax.dynamic_slice_in_dim(norm_gain, member * width, width, 0)[:, None]
    x = swap(outgoing, "seq")
    numer, denom, states, conv, weight_local = call(
        lambda *refs: forward_kernel(heads, *refs),
        "forward",
        [
            ((width, all_tokens), f32),
            ((8, all_tokens), f32),
            ((3 * LANES, heads * FEAT), bf16),
            ((width, all_tokens), bf16),
            ((width, features_out), bf16),
        ],
        (x, taps, seeds[None], out_weight),
    )
    weight_all = lax.all_gather(weight_local, "seq", axis=0, tiled=True)
    grad_normed, sums = call(
        lambda *refs: sums_kernel(heads, *refs),
        "sums",
        [((width, all_tokens), f32), ((groups, 2 * groups, LANES), f32)],
        (numer, denom, out_weight, cotangent_all, gain),
    )
    sums = swap(sums, "seq")
    normed, grad, weight_tiles, gain_part = call(
        lambda *refs: normed_kernel(heads, *refs),
        "normed",
        [
            ((groups, width, LANES), bf16),
            ((width, all_tokens), f32),
            ((1024, LANES), f32),
            ((width, LANES), f32),
        ],
        (numer, denom, grad_normed, sums, gain, cotangent_all),
    )
    weight_parts = swap(weight_tiles.reshape(packs, 1024 // packs, LANES), "dp")
    leaving, small = call(
        lambda *refs: backward_kernel(heads, *refs),
        "backward",
        [((groups, 4 * width + 16, LANES), bf16), ((16, LANES), f32)],
        (x, taps, seeds[None], seeds[:, None], numer, denom, states, conv, normed, grad, gain_part),
        scratch=[pltpu.VMEM((width, all_tokens), f32)],
    )
    shared = call(
        pack_sum_kernel,
        "pack_sum",
        [((packs, 1024 // packs + 16, LANES), f32)],
        (weight_parts, small),
    )[0]
    gathered = swap(shared, "dp")
    weight_grad, leaving = call(
        unpack_kernel,
        "unpack",
        [((width, features_out), f32), (leaving.shape, bf16)],
        (gathered, leaving),
        grid=(1,),
        in_specs=[
            pl.BlockSpec(gathered.shape, lambda i: (0, 0, 0)),
            pl.BlockSpec(memory_space=pl.ANY),
        ],
        out_specs=[
            pl.BlockSpec((width, features_out), lambda i: (0, 0)),
            pl.BlockSpec((groups, 16, LANES), lambda i: (0, 4 * width // 16, 0)),
        ],
        input_output_aliases={1: 1},
    )
    back = swap(leaving, "seq")
    normed_rows = back[:, :width].reshape(width_all, tokens)
    block_out = lax.dot_general(
        normed_rows, weight_all, (((0,), (0,)), ((), ())), preferred_element_type=f32
    ).astype(bf16)
    grads = back[:, width : 4 * width].reshape(groups, 3, width, tokens)
    grad_tokens = grads.transpose(3, 1, 0, 2).reshape(tokens, 3, width_all)
    small_all = back[:, 4 * width : 4 * width + 10, :width].astype(f32)
    small_all = small_all.transpose(1, 0, 2).reshape(10, width_all)
    return block_out[None], grad_tokens[None], weight_grad, small_all[9], small_all[:9]


def solution(mesh):
    in_specs = (
        P("dp", "seq", None, None),
        P("dp", "seq", None),
        P("seq", None),
        P(),
        P(),
        P(),
        P("dp", None, "seq"),
    )
    out_specs = (P("dp", "seq", None), P("dp", "seq", None, None), P("seq", None), P(), P())
    return jax.shard_map(local, mesh=mesh, in_specs=in_specs, out_specs=out_specs, check_vma=False)
```

```python
import math

import jax
import jax.numpy as jnp
from jax import lax
from jax.experimental import pallas as pl
from jax.experimental.pallas import tpu as pltpu
from jax.sharding import PartitionSpec as P

HEAD = 32
FEAT = 256
LANES = 128
CHUNK = 256
VMEM = 24 * 1024 * 1024
ALL_VMEM = 60 * 1024 * 1024
WIDTHS = (16, 32, 48, 64)

feature_floor = 0.1
epsilon = 1e-06
scale = 1.0 / math.sqrt(HEAD)
bf16, f32 = jnp.bfloat16, jnp.float32


def dot(a, b):
    return lax.dot_general(a, b, (((1,), (0,)), ((), ())), preferred_element_type=f32)


def dot_nt(a, b):
    return lax.dot_general(a, b, (((1,), (1,)), ((), ())), preferred_element_type=f32)


def omega_of(seed, e, f):
    hashed = seed * -1640531535 + (e * FEAT + f)
    hashed = hashed ^ ((hashed >> 16) & 65535)
    hashed = hashed * -2048144789
    hashed = hashed ^ ((hashed >> 13) & 524287)
    hashed = hashed * -1028477387
    hashed = hashed ^ ((hashed >> 16) & 65535)
    uniform = ((hashed >> 8) & 16777215).astype(f32) * (1.0 / 16777216.0)
    return 1.7320508 * (2.0 * uniform - 1.0)


def omega_tall(seed_row, heads):
    shape = (FEAT, heads * HEAD)
    lane = lax.broadcasted_iota(jnp.int32, shape, 1)
    block = omega_of(seed_row, lane % HEAD, lax.broadcasted_iota(jnp.int32, shape, 0))
    return jnp.concatenate(
        [jnp.where(lane // HEAD == h, block, 0.0) for h in range(heads)], axis=0
    ).astype(bf16)


def omega_wide(seed_column, heads):
    shape = (heads * HEAD, FEAT)
    row = lax.broadcasted_iota(jnp.int32, shape, 0)
    block = omega_of(seed_column, row % HEAD, lax.broadcasted_iota(jnp.int32, shape, 1))
    return jnp.concatenate(
        [jnp.where(row // HEAD == h, block, 0.0) for h in range(heads)], axis=1
    ).astype(bf16)


def head_mask(heads):
    shape = (LANES, heads * FEAT)
    row = lax.broadcasted_iota(jnp.int32, shape, 0)
    column = lax.broadcasted_iota(jnp.int32, shape, 1) // FEAT
    width = heads * HEAD
    channel = (row < width) & (row // HEAD == column)
    total = (row >= width) & (row < width + 3 * heads) & ((row - width) % heads == column)
    return channel | total


def chunk_of(ref, part, width, j):
    rows = pl.ds(part * width, width)
    return jnp.concatenate([ref[2 * j, rows, :], ref[2 * j + 1, rows, :]], axis=1)


def part_of(ref, start, count):
    return jnp.concatenate(
        [ref[s, pl.ds(start, count), :] for s in range(ref.shape[0])], axis=1
    )


def by_head(rows, heads):
    return jnp.concatenate(
        [jnp.broadcast_to(rows[h : h + 1], (HEAD, rows.shape[1])) for h in range(heads)], axis=0
    )


def head_sums(values, heads):
    return [
        jnp.sum(values[h * HEAD : (h + 1) * HEAD], axis=0, keepdims=True) for h in range(heads)
    ]


def shifted(values, shift):
    return pltpu.roll(values, shift % values.shape[1], axis=1)


class Grid:
    def __init__(self, ref, start):
        packing = part_of(ref, start, 16).astype(f32)
        self.image, self.row, self.column, self.width, self.height = (
            packing[i : i + 1] for i in range(5)
        )
        self.left = self.column > 0.5
        self.right = self.column < self.width - 1.5
        self.above = self.row > 0.5
        self.below = self.row < self.height - 1.5

    def column_before(self, values):
        return jnp.where(self.left, shifted(values, 1), 0.0)

    def column_after(self, values):
        return jnp.where(self.right, shifted(values, -1), 0.0)

    def by_rows(self, values, inside, sign):
        half = values.shape[1] // 2
        moved = jnp.where(inside & (self.width == 16.0), shifted(values, sign * 16), 0.0)
        front, back = moved[:, :half], moved[:, half:]
        for width in WIDTHS[1:]:
            mask = inside[:, :half] & (self.width[:, :half] == float(width))
            front = front + jnp.where(mask, shifted(values[:, :half], sign * width), 0.0)
        return jnp.concatenate([front, back], axis=1)

    def row_above(self, values):
        return self.by_rows(values, self.above, 1)

    def row_below(self, values):
        return self.by_rows(values, self.below, -1)


def features(pre):
    return (jnp.maximum(pre, 0.0) + feature_floor).astype(bf16)


def split_images(rows, image, j, middle):
    zero = jnp.zeros((), rows.dtype)
    front = back = None
    if j < middle:
        front = jnp.concatenate(
            [jnp.where(image == 0.0, rows, zero), jnp.where(image == 1.0, rows, zero)], axis=0
        ).astype(bf16)
    if j >= middle - 1:
        back = jnp.where(image == 2.0, rows, zero).astype(bf16)
    return front, back


def add(total, term):
    return term if total is None else total + term


def pick_image(left, right, image, j, middle, rows):
    if j < middle - 1:
        both = dot(left[: 2 * LANES], right)
        return jnp.where(image == 0.0, both[:rows], both[LANES : LANES + rows])
    if j >= middle:
        return dot(left[2 * LANES :], right)[:rows]
    every = dot(left, right)
    front = jnp.where(image == 0.0, every[:rows], every[LANES : LANES + rows])
    return jnp.where(image == 2.0, every[2 * LANES : 2 * LANES + rows], front)


def ones_rows(width, columns, count):
    row = lax.broadcasted_iota(jnp.int32, (LANES - width, columns), 0)
    return jnp.where(row < count, 1.0, 0.0)


def prepare_kernel(projected_ref, packing_ref, out_ref):
    groups = out_ref.shape[0]
    parts, tokens, width_all = projected_ref.shape
    width = width_all // groups
    for part in range(parts):
        turned = jnp.transpose(projected_ref[part])
        for g in range(groups):
            out_ref[g, pl.ds(part * width, width), :] = turned[g * width : (g + 1) * width]
    rows = packing_ref[...].astype(f32).astype(bf16)
    for g in range(groups):
        out_ref[g, pl.ds(parts * width, 16), :] = rows


def finish_kernel(normed_ref, grad_ref, weight_ref, block_ref, grad_out):
    groups, width, tokens = normed_ref.shape
    grad_out[0] = jnp.transpose(grad_ref[...].reshape(groups * width, tokens))
    normed = jnp.transpose(normed_ref[...].reshape(groups * width, tokens))
    block_ref[...] = dot(normed, weight_ref[...]).astype(bf16)


def forward_kernel(heads, x_ref, taps_ref, seed_row_ref, weight_ref,
                   numer_ref, denom_ref, attention_ref, squares_ref, states_ref, conv_ref, weight_out):
    width = heads * HEAD
    chunks = x_ref.shape[0] * LANES // CHUNK
    middle = chunks // 2
    weight_out[...] = weight_ref[...]
    grid = Grid(x_ref, 3 * width)
    values = part_of(x_ref, 2 * width, width).astype(f32)
    taps = taps_ref[...]
    trio = (grid.column_before(values), values, grid.column_after(values))

    def row_of_taps(r):
        return sum(taps[:, 3 * r + c : 3 * r + c + 1] * trio[c] for c in range(3))

    conv = row_of_taps(1) + grid.row_above(row_of_taps(0)) + grid.row_below(row_of_taps(2))
    conv_ref[...] = conv.astype(bf16)
    omega = omega_tall(seed_row_ref[...], heads)
    front = back = None
    for j in range(chunks):
        lanes = pl.ds(j * CHUNK, CHUNK)
        image = grid.image[:, j * CHUNK : (j + 1) * CHUNK]
        rows = jnp.concatenate(
            [conv_ref[:, lanes].astype(f32), ones_rows(width, CHUNK, 3 * heads)], axis=0
        )
        feat_key = features(dot(omega, chunk_of(x_ref, 1, width, j)) * scale)
        first, last = split_images(rows, image, j, middle)
        if first is not None:
            front = add(front, dot_nt(first, feat_key))
        if last is not None:
            back = add(back, dot_nt(last, feat_key))
    mask = head_mask(heads)
    states = jnp.concatenate(
        [
            jnp.where(mask, part, 0.0).astype(bf16)
            for part in (front[:LANES], front[LANES:], back)
        ],
        axis=0,
    )
    states_ref[...] = states
    squares = []
    for j in range(chunks):
        lanes = pl.ds(j * CHUNK, CHUNK)
        image = grid.image[:, j * CHUNK : (j + 1) * CHUNK]
        feat_query = features(dot(omega, chunk_of(x_ref, 0, width, j)) * scale)
        both = pick_image(states, feat_query, image, j, middle, width + 8)
        numer_ref[:, lanes] = both[:width]
        denom_ref[:, lanes] = both[width : width + 8]
        attention = (both[:width] / by_head(both[width : width + 8], heads)).astype(bf16)
        attention_ref[:, lanes] = attention
        attention = attention.astype(f32)
        squares.append(jnp.sum(attention * attention, axis=0, keepdims=True))
    to_peers(squares, squares_ref)


def to_peers(sums, out_ref):
    rows = [
        total[:, part * LANES : (part + 1) * LANES]
        for total in sums
        for part in range(CHUNK // LANES)
    ]
    rows = jnp.concatenate(rows, axis=0).astype(bf16)
    for peer in range(out_ref.shape[0]):
        out_ref[peer] = rows


def tokens_of(values, j):
    return jnp.concatenate([values[2 * j : 2 * j + 1], values[2 * j + 1 : 2 * j + 2]], axis=1)


def inner_kernel(attention_ref, weight_ref, cotangent_ref, gain_ref, grad_normed_ref, inner_ref,
                 rows_ref):
    step = pl.program_id(0)
    chunks = attention_ref.shape[1] // CHUNK
    weight, gain = weight_ref[...], gain_ref[...]
    rows = []
    for j in range(chunks):
        lanes = pl.ds(j * CHUNK, CHUNK)
        grad_normed = dot_nt(weight, cotangent_ref[pl.ds(j * CHUNK, CHUNK), :])
        grad_normed_ref[:, lanes] = grad_normed
        attention = attention_ref[:, lanes].astype(f32)
        inner = jnp.sum(gain * grad_normed * attention, axis=0, keepdims=True)
        for part in range(CHUNK // LANES):
            rows.append(inner[:, part * LANES : (part + 1) * LANES])
    rows_ref[pl.ds(pl.multiple_of(step * 8, 8), 8), :] = jnp.concatenate(rows, axis=0)

    @pl.when(step == pl.num_programs(0) - 1)
    def _():
        rows = rows_ref[...].astype(bf16)
        for peer in range(inner_ref.shape[0]):
            inner_ref[peer] = rows


def normed_kernel(attention_ref, grad_normed_ref, squares_ref, gain_ref, cotangent_ref,
                  normed_ref, inverse_ref, weight_ref, gain_out):
    width, tokens = attention_ref.shape
    chunks = tokens // CHUNK
    groups = squares_ref.shape[0]
    gain = gain_ref[...]
    squares = jnp.sum(squares_ref[...].astype(f32), axis=0)
    inverse = lax.rsqrt(squares * (1.0 / (width * groups)) + epsilon)
    inverse_ref[...] = inverse
    weight = gain_sum = None
    for j in range(chunks):
        lanes = pl.ds(j * CHUNK, CHUNK)
        inv_rms = tokens_of(inverse, j)
        attention = attention_ref[:, lanes].astype(f32)
        normed = (attention * gain * inv_rms).astype(bf16)
        gain_sum = add(gain_sum, grad_normed_ref[:, lanes] * attention * inv_rms)
        for part in range(CHUNK // LANES):
            normed_ref[2 * j + part] = normed[:, part * LANES : (part + 1) * LANES]
        weight = add(weight, dot(normed, cotangent_ref[pl.ds(j * CHUNK, CHUNK), :]))
    gain_out[...] = jnp.broadcast_to(jnp.sum(gain_sum, axis=1, keepdims=True), gain_out.shape)
    across = weight.shape[1] // LANES
    weight = weight.astype(bf16)
    for r in range(width // 16):
        for c in range(across):
            weight_ref[pl.ds((r * across + c) * 16, 16), :] = weight[
                r * 16 : (r + 1) * 16, c * LANES : (c + 1) * LANES
            ]
    used = width * across
    weight_ref[used:, :] = jnp.zeros((weight_ref.shape[0] - used, LANES), bf16)


def backward_kernel(heads, x_ref, taps_ref, seed_row_ref, seed_column_ref, numer_ref, denom_ref,
                    states_ref, conv_ref, normed_ref, attention_ref, grad_normed_ref,
                    inverse_ref, inner_ref, norm_gain_ref, gain_ref, out_ref, small_ref, grad_conv_ref):
    width = heads * HEAD
    chunks = x_ref.shape[0] * LANES // CHUNK
    middle = chunks // 2
    grid = Grid(x_ref, 3 * width)
    omega = omega_tall(seed_row_ref[...], heads)
    omega_back = omega_wide(seed_column_ref[...], heads)
    states = jnp.transpose(states_ref[...].astype(f32)).astype(bf16)
    mask = head_mask(heads)
    front = back = None
    norm_gain = norm_gain_ref[...]
    inverse = inverse_ref[...]
    away = jnp.sum(inner_ref[...].astype(f32), axis=0) * (1.0 / (width * x_ref.shape[0]))
    away = inverse * inverse * inverse * away

    def put(part, j, values):
        for half in range(CHUNK // LANES):
            out_ref[2 * j + half, pl.ds(part * width, width), :] = values[
                :, half * LANES : (half + 1) * LANES
            ]

    def spread(table, first, last):
        total = None
        if first is not None:
            total = add(total, dot(table[:, : 2 * LANES], first))
        if last is not None:
            total = add(total, dot(table[:, 2 * LANES :], last))
        return total

    for j in range(chunks):
        lanes = pl.ds(j * CHUNK, CHUNK)
        image = grid.image[:, j * CHUNK : (j + 1) * CHUNK]
        pre = dot(omega, chunk_of(x_ref, 0, width, j)) * scale
        feat_query = features(pre)
        grad = tokens_of(inverse, j) * norm_gain * grad_normed_ref[:, lanes]
        grad = grad - attention_ref[:, lanes].astype(f32) * tokens_of(away, j)
        grad = grad.astype(bf16).astype(f32)
        denom = denom_ref[:, lanes]
        grad_numer = (grad / by_head(denom, heads)).astype(bf16).astype(f32)
        dots = head_sums(grad * numer_ref[:, lanes], heads)
        row = lax.broadcasted_iota(jnp.int32, (LANES - width, CHUNK), 0)
        extra = jnp.zeros((LANES - width, CHUNK), f32)
        for h in range(heads):
            below = denom[h : h + 1]
            rest = -dots[h] / (below * below)
            for level in range(3):
                high = rest.astype(bf16).astype(f32)
                extra = jnp.where(row == level * heads + h, high, extra)
                rest = rest - high
        rows = jnp.concatenate([grad_numer, extra], axis=0)
        first, last = split_images(rows, image, j, middle)
        if first is not None:
            front = add(front, dot_nt(first, feat_query))
        if last is not None:
            back = add(back, dot_nt(last, feat_query))
        gate = jnp.where(pre > 0, spread(states, first, last), 0.0).astype(bf16)
        put(1, j, (dot(omega_back, gate) * scale).astype(bf16))
    parts = []
    for part in (front[:LANES], front[LANES:], back):
        part = jnp.where(mask, part, 0.0)
        total = jnp.sum(part[width:], axis=0, keepdims=True)
        row = lax.broadcasted_iota(jnp.int32, (LANES - width, heads * FEAT), 0)
        parts.append(part[:width])
        parts.append(jnp.where(row == 0, total, 0.0))
    grad_states = jnp.concatenate(parts, axis=0)
    table = jnp.transpose(grad_states).astype(bf16)
    grad_states = grad_states.astype(bf16)
    for j in range(chunks):
        lanes = pl.ds(j * CHUNK, CHUNK)
        image = grid.image[:, j * CHUNK : (j + 1) * CHUNK]
        pre = dot(omega, chunk_of(x_ref, 1, width, j)) * scale
        feat_key = features(pre)
        rows = jnp.concatenate(
            [conv_ref[:, lanes].astype(f32), ones_rows(width, CHUNK, 1)], axis=0
        )
        first, last = split_images(rows, image, j, middle)
        gate = jnp.where(pre > 0, spread(table, first, last), 0.0).astype(bf16)
        put(2, j, (dot(omega_back, gate) * scale).astype(bf16))
        grad_conv_ref[:, lanes] = (
            pick_image(grad_states, feat_key, image, j, middle, width).astype(bf16).astype(f32)
        )
    grad_conv = grad_conv_ref[...]
    values = part_of(x_ref, 2 * width, width).astype(f32)
    taps = taps_ref[...]
    trio = (grid.column_before(values), values, grid.column_after(values))
    moved = (grid.row_below(grad_conv), grad_conv, grid.row_above(grad_conv))
    lane = lax.broadcasted_iota(jnp.int32, (width, LANES), 1)
    small = jnp.where(lane == 9, gain_ref[...], 0.0)
    for r in range(3):
        for c in range(3):
            total = jnp.sum(moved[r] * trio[c], axis=1, keepdims=True)
            small = jnp.where(lane == 3 * r + c, total, small)

    def column_of_taps(c):
        return sum(taps[:, 3 * r + c : 3 * r + c + 1] * moved[r] for r in range(3))

    grad_values = (
        column_of_taps(1)
        + grid.column_after(column_of_taps(0))
        + grid.column_before(column_of_taps(2))
    ).astype(bf16)
    small = jnp.concatenate([small, jnp.zeros((LANES - width, LANES), f32)], axis=0)
    small_ref[...] = jnp.transpose(small)[: small_ref.shape[0]]
    for s in range(x_ref.shape[0]):
        out_ref[s, pl.ds(0, width), :] = normed_ref[s]
        out_ref[s, pl.ds(3 * width, width), :] = grad_values[:, s * LANES : (s + 1) * LANES]
        out_ref[s, pl.ds(4 * width, 16), :] = jnp.zeros((16, LANES), bf16)


def pack_sum_kernel(parts_ref, small_ref, out_ref):
    packs = parts_ref.shape[0]
    rows = parts_ref.shape[1]
    total = (jnp.sum(parts_ref[...].astype(f32), axis=0) * (1.0 / packs)).astype(bf16)
    small = small_ref[...].astype(bf16)
    for peer in range(packs):
        out_ref[peer, pl.ds(0, rows), :] = total
        out_ref[peer, pl.ds(rows, 16), :] = small


def small_kernel(gathered_ref, outgoing_ref, payload_ref):
    packs = gathered_ref.shape[0]
    small = jnp.sum(gathered_ref[...].astype(f32), axis=0) * (1.0 / packs)
    for peer in range(payload_ref.shape[0]):
        payload_ref[peer] = small.astype(bf16)


def unpack_kernel(gathered_ref, weight_ref):
    rows = gathered_ref.shape[1] - 16
    width, features_out = weight_ref.shape
    across = features_out // LANES
    for r in range(width // 16):
        for c in range(across):
            start = (r * across + c) * 16
            weight_ref[pl.ds(r * 16, 16), pl.ds(c * LANES, LANES)] = gathered_ref[
                start // rows, pl.ds(start % rows, 16), :
            ].astype(f32)


def call(kernel, name, out_shapes, operands, scratch=(), vmem=VMEM, **more):
    return pl.pallas_call(
        kernel,
        name=name,
        out_shape=[jax.ShapeDtypeStruct(shape, kind) for shape, kind in out_shapes],
        scratch_shapes=list(scratch),
        compiler_params=pltpu.CompilerParams(vmem_limit_bytes=vmem),
        **more,
    )(*operands)


def swap(blocks, axis):
    return lax.all_to_all(blocks, axis, split_axis=0, concat_axis=0, tiled=True)


def local(projected, cotangent, out_weight, norm_gain, conv_taps, feature_seeds, packing):
    groups = lax.axis_size("seq")
    member = lax.axis_index("seq")
    packs = lax.axis_size("dp")
    tokens, _, width_all = projected.shape[1:]
    features_out = cotangent.shape[2]
    width = width_all // groups
    heads = width // HEAD
    all_tokens = tokens * groups
    cotangent_all = lax.all_gather(cotangent[0], "seq", axis=0, tiled=True)
    outgoing = call(
        prepare_kernel,
        "prepare",
        [((groups, 3 * width + 16, tokens), bf16)],
        (projected[0].transpose(1, 0, 2), jnp.pad(packing[0], ((0, 11), (0, 0)))),
    )[0]
    seeds = jnp.repeat(lax.dynamic_slice_in_dim(feature_seeds, member * heads, heads, 0), HEAD)
    taps = jnp.pad(
        lax.dynamic_slice_in_dim(conv_taps, member * width, width, 1).T, ((0, 0), (0, 7))
    )
    gain = lax.dynamic_slice_in_dim(norm_gain, member * width, width, 0)[:, None]
    x = swap(outgoing, "seq")
    numer, denom, attention, squares, states, conv, weight_local = call(
        lambda *refs: forward_kernel(heads, *refs),
        "forward",
        [
            ((width, all_tokens), f32),
            ((8, all_tokens), f32),
            ((width, all_tokens), bf16),
            ((groups, groups, LANES), bf16),
            ((3 * LANES, heads * FEAT), bf16),
            ((width, all_tokens), bf16),
            ((width, features_out), bf16),
        ],
        (x, taps, seeds[None], out_weight),
    )
    squares = swap(squares, "seq")
    weight_all = lax.all_gather(weight_local, "seq", axis=0, tiled=True)
    grad_normed, inner = call(
        inner_kernel,
        "inner",
        [((width, all_tokens), f32), ((groups, groups, LANES), bf16)],
        (attention, out_weight, cotangent_all, gain),
        vmem=ALL_VMEM,
        grid=(groups // 8,),
        in_specs=[
            pl.BlockSpec((width, 8 * LANES), lambda i: (0, i)),
            pl.BlockSpec((width, features_out), lambda i: (0, 0)),
            pl.BlockSpec((8 * LANES, features_out), lambda i: (i, 0)),
            pl.BlockSpec((width, 1), lambda i: (0, 0)),
        ],
        out_specs=[
            pl.BlockSpec((width, 8 * LANES), lambda i: (0, i)),
            pl.BlockSpec((groups, groups, LANES), lambda i: (0, 0, 0)),
        ],
        scratch=[pltpu.VMEM((groups, LANES), f32)],
    )
    inner = swap(inner, "seq")
    normed, inverse, weight_tiles, gain_part = call(
        normed_kernel,
        "normed",
        [
            ((groups, width, LANES), bf16),
            ((groups, LANES), f32),
            ((1024, LANES), bf16),
            ((width, LANES), f32),
        ],
        (attention, grad_normed, squares, gain, cotangent_all),
    )
    weight_parts = swap(weight_tiles.reshape(packs, 1024 // packs, LANES), "dp")
    leaving, small = call(
        lambda *refs: backward_kernel(heads, *refs),
        "backward",
        [((groups, 4 * width + 16, LANES), bf16), ((16, LANES), f32)],
        (x, taps, seeds[None], seeds[:, None], numer, denom, states, conv, normed, attention,
         grad_normed, inverse, inner, gain, gain_part),
        scratch=[pltpu.VMEM((width, all_tokens), f32)],
    )
    shared = call(
        pack_sum_kernel,
        "pack_sum",
        [((packs, 1024 // packs + 16, LANES), bf16)],
        (weight_parts, small),
    )[0]
    gathered = swap(shared, "dp")
    leaving = call(
        small_kernel,
        "small",
        [(leaving.shape, bf16)],
        (gathered, leaving),
        grid=(1,),
        in_specs=[
            pl.BlockSpec((packs, 16, LANES), lambda i: (0, 1024 // packs // 16, 0)),
            pl.BlockSpec(memory_space=pl.ANY),
        ],
        out_specs=[pl.BlockSpec((groups, 16, LANES), lambda i: (0, 4 * width // 16, 0))],
        input_output_aliases={1: 0},
    )[0]
    weight_grad = call(
        unpack_kernel, "unpack", [((width, features_out), f32)], (gathered,)
    )[0]
    back = swap(leaving, "seq")
    across = features_out // 3
    block_out, grads = call(
        finish_kernel,
        "finish",
        [((tokens, features_out), bf16), ((3, tokens, width_all), bf16)],
        (back, back, weight_all),
        vmem=ALL_VMEM,
        grid=(3,),
        in_specs=[
            pl.BlockSpec((groups, width, tokens), lambda i: (0, 0, 0)),
            pl.BlockSpec((groups, width, tokens), lambda i: (0, i + 1, 0)),
            pl.BlockSpec((width_all, across), lambda i: (0, i)),
        ],
        out_specs=[
            pl.BlockSpec((tokens, across), lambda i: (0, i)),
            pl.BlockSpec((1, tokens, width_all), lambda i: (i, 0, 0)),
        ],
    )
    grad_tokens = grads.transpose(1, 0, 2)
    small_all = back[:, 4 * width : 4 * width + 10, :width].astype(f32)
    small_all = small_all.transpose(1, 0, 2).reshape(10, width_all)
    return block_out[None], grad_tokens[None], weight_grad, small_all[9], small_all[:9]


def solution(mesh):
    in_specs = (
        P("dp", "seq", None, None),
        P("dp", "seq", None),
        P("seq", None),
        P(),
        P(),
        P(),
        P("dp", None, "seq"),
    )
    out_specs = (P("dp", "seq", None), P("dp", "seq", None, None), P("seq", None), P(), P())
    return jax.shard_map(local, mesh=mesh, in_specs=in_specs, out_specs=out_specs, check_vma=False)
```

```python
import math

import jax
import jax.numpy as jnp
from jax import lax
from jax.experimental import pallas as pl
from jax.experimental.pallas import tpu as pltpu
from jax.sharding import PartitionSpec as P

HEAD = 32
FEAT = 256
LANES = 128
CHUNK = 256
VMEM = 24 * 1024 * 1024
ALL_VMEM = 60 * 1024 * 1024
WIDTHS = (16, 32, 48, 64)

feature_floor = 0.1
epsilon = 1e-06
scale = 1.0 / math.sqrt(HEAD)
bf16, f32 = jnp.bfloat16, jnp.float32


def dot(a, b):
    return lax.dot_general(a, b, (((1,), (0,)), ((), ())), preferred_element_type=f32)


def dot_nt(a, b):
    return lax.dot_general(a, b, (((1,), (1,)), ((), ())), preferred_element_type=f32)


def omega_of(seed, e, f):
    hashed = seed * -1640531535 + (e * FEAT + f)
    hashed = hashed ^ ((hashed >> 16) & 65535)
    hashed = hashed * -2048144789
    hashed = hashed ^ ((hashed >> 13) & 524287)
    hashed = hashed * -1028477387
    hashed = hashed ^ ((hashed >> 16) & 65535)
    uniform = ((hashed >> 8) & 16777215).astype(f32) * (1.0 / 16777216.0)
    return 1.7320508 * (2.0 * uniform - 1.0)


def omega_tall(seed_row, heads):
    shape = (FEAT, heads * HEAD)
    lane = lax.broadcasted_iota(jnp.int32, shape, 1)
    block = omega_of(seed_row, lane % HEAD, lax.broadcasted_iota(jnp.int32, shape, 0))
    return jnp.concatenate(
        [jnp.where(lane // HEAD == h, block, 0.0) for h in range(heads)], axis=0
    ).astype(bf16)


def omega_wide(seed_column, heads):
    shape = (heads * HEAD, FEAT)
    row = lax.broadcasted_iota(jnp.int32, shape, 0)
    block = omega_of(seed_column, row % HEAD, lax.broadcasted_iota(jnp.int32, shape, 1))
    return jnp.concatenate(
        [jnp.where(row // HEAD == h, block, 0.0) for h in range(heads)], axis=1
    ).astype(bf16)


def head_mask(heads):
    shape = (LANES, heads * FEAT)
    row = lax.broadcasted_iota(jnp.int32, shape, 0)
    column = lax.broadcasted_iota(jnp.int32, shape, 1) // FEAT
    width = heads * HEAD
    channel = (row < width) & (row // HEAD == column)
    total = (row >= width) & (row < width + 3 * heads) & ((row - width) % heads == column)
    return channel | total


def chunk_of(ref, part, width, j):
    rows = pl.ds(part * width, width)
    return jnp.concatenate([ref[2 * j, rows, :], ref[2 * j + 1, rows, :]], axis=1)


def part_of(ref, start, count):
    return jnp.concatenate(
        [ref[s, pl.ds(start, count), :] for s in range(ref.shape[0])], axis=1
    )


def by_head(rows, heads):
    return jnp.concatenate(
        [jnp.broadcast_to(rows[h : h + 1], (HEAD, rows.shape[1])) for h in range(heads)], axis=0
    )


def head_sums(values, heads):
    return [
        jnp.sum(values[h * HEAD : (h + 1) * HEAD], axis=0, keepdims=True) for h in range(heads)
    ]


def shifted(values, shift):
    return pltpu.roll(values, shift % values.shape[1], axis=1)


class Grid:
    def __init__(self, ref, start):
        packing = part_of(ref, start, 16).astype(f32)
        self.image, self.row, self.column, self.width, self.height = (
            packing[i : i + 1] for i in range(5)
        )
        self.left = self.column > 0.5
        self.right = self.column < self.width - 1.5
        self.above = self.row > 0.5
        self.below = self.row < self.height - 1.5

    def column_before(self, values):
        return jnp.where(self.left, shifted(values, 1), 0.0)

    def column_after(self, values):
        return jnp.where(self.right, shifted(values, -1), 0.0)

    def by_rows(self, values, inside, sign):
        half = values.shape[1] // 2
        moved = jnp.where(inside & (self.width == 16.0), shifted(values, sign * 16), 0.0)
        front, back = moved[:, :half], moved[:, half:]
        for width in WIDTHS[1:]:
            mask = inside[:, :half] & (self.width[:, :half] == float(width))
            front = front + jnp.where(mask, shifted(values[:, :half], sign * width), 0.0)
        return jnp.concatenate([front, back], axis=1)

    def row_above(self, values):
        return self.by_rows(values, self.above, 1)

    def row_below(self, values):
        return self.by_rows(values, self.below, -1)


def features(pre):
    return (jnp.maximum(pre, 0.0) + feature_floor).astype(bf16)


def split_images(rows, image, j, middle):
    zero = jnp.zeros((), rows.dtype)
    front = back = None
    if j < middle:
        front = jnp.concatenate(
            [jnp.where(image == 0.0, rows, zero), jnp.where(image == 1.0, rows, zero)], axis=0
        ).astype(bf16)
    if j >= middle - 1:
        back = jnp.where(image == 2.0, rows, zero).astype(bf16)
    return front, back


def add(total, term):
    return term if total is None else total + term


def pick_image(left, right, image, j, middle, rows):
    if j < middle - 1:
        both = dot(left[: 2 * LANES], right)
        return jnp.where(image == 0.0, both[:rows], both[LANES : LANES + rows])
    if j >= middle:
        return dot(left[2 * LANES :], right)[:rows]
    every = dot(left, right)
    front = jnp.where(image == 0.0, every[:rows], every[LANES : LANES + rows])
    return jnp.where(image == 2.0, every[2 * LANES : 2 * LANES + rows], front)


def ones_rows(width, columns, count):
    row = lax.broadcasted_iota(jnp.int32, (LANES - width, columns), 0)
    return jnp.where(row < count, 1.0, 0.0)


def prepare_kernel(projected_ref, packing_ref, out_ref):
    groups = out_ref.shape[0]
    parts, tokens, width_all = projected_ref.shape
    width = width_all // groups
    for part in range(parts):
        turned = jnp.transpose(projected_ref[part])
        for g in range(groups):
            out_ref[g, pl.ds(part * width, width), :] = turned[g * width : (g + 1) * width]
    rows = packing_ref[...].astype(f32).astype(bf16)
    for g in range(groups):
        out_ref[g, pl.ds(parts * width, 16), :] = rows


def finish_kernel(normed_ref, grad_ref, weight_ref, block_ref, grad_out, turned_ref):
    groups, width, tokens = normed_ref.shape

    @pl.when(pl.program_id(0) == 0)
    def _():
        turned_ref[...] = jnp.transpose(normed_ref[...].reshape(groups * width, tokens))

    grad_out[0] = jnp.transpose(grad_ref[...].reshape(groups * width, tokens))
    block_ref[...] = dot(turned_ref[...], weight_ref[...]).astype(bf16)


def forward_kernel(heads, x_ref, taps_ref, seed_row_ref, weight_ref,
                   numer_ref, denom_ref, attention_ref, squares_ref, states_ref, conv_ref, weight_out):
    width = heads * HEAD
    chunks = x_ref.shape[0] * LANES // CHUNK
    middle = chunks // 2
    weight_out[...] = weight_ref[...]
    grid = Grid(x_ref, 3 * width)
    values = part_of(x_ref, 2 * width, width).astype(f32)
    taps = taps_ref[...]
    trio = (grid.column_before(values), values, grid.column_after(values))

    def row_of_taps(r):
        return sum(taps[:, 3 * r + c : 3 * r + c + 1] * trio[c] for c in range(3))

    conv = row_of_taps(1) + grid.row_above(row_of_taps(0)) + grid.row_below(row_of_taps(2))
    conv_ref[...] = conv.astype(bf16)
    omega = omega_tall(seed_row_ref[...], heads)
    front = back = None
    for j in range(chunks):
        lanes = pl.ds(j * CHUNK, CHUNK)
        image = grid.image[:, j * CHUNK : (j + 1) * CHUNK]
        rows = jnp.concatenate(
            [conv_ref[:, lanes].astype(f32), ones_rows(width, CHUNK, 3 * heads)], axis=0
        )
        feat_key = features(dot(omega, chunk_of(x_ref, 1, width, j)) * scale)
        first, last = split_images(rows, image, j, middle)
        if first is not None:
            front = add(front, dot_nt(first, feat_key))
        if last is not None:
            back = add(back, dot_nt(last, feat_key))
    mask = head_mask(heads)
    states = jnp.concatenate(
        [
            jnp.where(mask, part, 0.0).astype(bf16)
            for part in (front[:LANES], front[LANES:], back)
        ],
        axis=0,
    )
    states_ref[...] = states
    squares = []
    for j in range(chunks):
        lanes = pl.ds(j * CHUNK, CHUNK)
        image = grid.image[:, j * CHUNK : (j + 1) * CHUNK]
        feat_query = features(dot(omega, chunk_of(x_ref, 0, width, j)) * scale)
        both = pick_image(states, feat_query, image, j, middle, width + 8)
        numer_ref[:, lanes] = both[:width]
        denom_ref[:, lanes] = both[width : width + 8]
        attention = (both[:width] / by_head(both[width : width + 8], heads)).astype(bf16)
        attention_ref[:, lanes] = attention
        attention = attention.astype(f32)
        squares.append(jnp.sum(attention * attention, axis=0, keepdims=True))
    to_peers(squares, squares_ref)


def to_peers(sums, out_ref):
    rows = [
        total[:, part * LANES : (part + 1) * LANES]
        for total in sums
        for part in range(CHUNK // LANES)
    ]
    rows = jnp.concatenate(rows, axis=0).astype(bf16)
    for peer in range(out_ref.shape[0]):
        out_ref[peer] = rows


def tokens_of(values, j):
    return jnp.concatenate([values[2 * j : 2 * j + 1], values[2 * j + 1 : 2 * j + 2]], axis=1)


def inner_kernel(attention_ref, weight_ref, cotangent_ref, gain_ref, grad_normed_ref, inner_ref,
                 rows_ref):
    step = pl.program_id(0)
    chunks = attention_ref.shape[1] // CHUNK
    weight, gain = weight_ref[...], gain_ref[...]
    rows = []
    for j in range(chunks):
        lanes = pl.ds(j * CHUNK, CHUNK)
        grad_normed = dot_nt(weight, cotangent_ref[pl.ds(j * CHUNK, CHUNK), :])
        grad_normed_ref[:, lanes] = grad_normed
        attention = attention_ref[:, lanes].astype(f32)
        inner = jnp.sum(gain * grad_normed * attention, axis=0, keepdims=True)
        for part in range(CHUNK // LANES):
            rows.append(inner[:, part * LANES : (part + 1) * LANES])
    rows_ref[pl.ds(pl.multiple_of(step * 8, 8), 8), :] = jnp.concatenate(rows, axis=0)

    @pl.when(step == pl.num_programs(0) - 1)
    def _():
        rows = rows_ref[...].astype(bf16)
        for peer in range(inner_ref.shape[0]):
            inner_ref[peer] = rows


def normed_kernel(attention_ref, grad_normed_ref, squares_ref, gain_ref, cotangent_ref,
                  normed_ref, inverse_ref, weight_ref, gain_out):
    width, tokens = attention_ref.shape
    chunks = tokens // CHUNK
    groups = squares_ref.shape[0]
    gain = gain_ref[...]
    squares = jnp.sum(squares_ref[...].astype(f32), axis=0)
    inverse = lax.rsqrt(squares * (1.0 / (width * groups)) + epsilon)
    inverse_ref[...] = inverse
    weight = gain_sum = None
    for j in range(chunks):
        lanes = pl.ds(j * CHUNK, CHUNK)
        inv_rms = tokens_of(inverse, j)
        attention = attention_ref[:, lanes].astype(f32)
        normed = (attention * gain * inv_rms).astype(bf16)
        gain_sum = add(gain_sum, grad_normed_ref[:, lanes] * attention * inv_rms)
        for part in range(CHUNK // LANES):
            normed_ref[2 * j + part] = normed[:, part * LANES : (part + 1) * LANES]
        weight = add(weight, dot(normed, cotangent_ref[pl.ds(j * CHUNK, CHUNK), :]))
    gain_out[...] = jnp.broadcast_to(jnp.sum(gain_sum, axis=1, keepdims=True), gain_out.shape)
    across = weight.shape[1] // LANES
    weight = weight.astype(bf16)
    for r in range(width // 16):
        for c in range(across):
            weight_ref[pl.ds((r * across + c) * 16, 16), :] = weight[
                r * 16 : (r + 1) * 16, c * LANES : (c + 1) * LANES
            ]
    used = width * across
    weight_ref[used:, :] = jnp.zeros((weight_ref.shape[0] - used, LANES), bf16)


def backward_kernel(heads, x_ref, taps_ref, seed_row_ref, seed_column_ref, numer_ref, denom_ref,
                    states_ref, conv_ref, normed_ref, attention_ref, grad_normed_ref,
                    inverse_ref, inner_ref, norm_gain_ref, gain_ref, out_ref, small_ref, grad_conv_ref):
    width = heads * HEAD
    chunks = x_ref.shape[0] * LANES // CHUNK
    middle = chunks // 2
    grid = Grid(x_ref, 3 * width)
    omega = omega_tall(seed_row_ref[...], heads)
    omega_back = omega_wide(seed_column_ref[...], heads)
    states = jnp.transpose(states_ref[...].astype(f32)).astype(bf16)
    mask = head_mask(heads)
    front = back = None
    norm_gain = norm_gain_ref[...]
    inverse = inverse_ref[...]
    away = jnp.sum(inner_ref[...].astype(f32), axis=0) * (1.0 / (width * x_ref.shape[0]))
    away = inverse * inverse * inverse * away

    def put(part, j, values):
        for half in range(CHUNK // LANES):
            out_ref[2 * j + half, pl.ds(part * width, width), :] = values[
                :, half * LANES : (half + 1) * LANES
            ]

    def spread(table, first, last):
        total = None
        if first is not None:
            total = add(total, dot(table[:, : 2 * LANES], first))
        if last is not None:
            total = add(total, dot(table[:, 2 * LANES :], last))
        return total

    for j in range(chunks):
        lanes = pl.ds(j * CHUNK, CHUNK)
        image = grid.image[:, j * CHUNK : (j + 1) * CHUNK]
        pre = dot(omega, chunk_of(x_ref, 0, width, j)) * scale
        feat_query = features(pre)
        grad = tokens_of(inverse, j) * norm_gain * grad_normed_ref[:, lanes]
        grad = grad - attention_ref[:, lanes].astype(f32) * tokens_of(away, j)
        grad = grad.astype(bf16).astype(f32)
        denom = denom_ref[:, lanes]
        grad_numer = (grad / by_head(denom, heads)).astype(bf16).astype(f32)
        dots = head_sums(grad * numer_ref[:, lanes], heads)
        row = lax.broadcasted_iota(jnp.int32, (LANES - width, CHUNK), 0)
        extra = jnp.zeros((LANES - width, CHUNK), f32)
        for h in range(heads):
            below = denom[h : h + 1]
            rest = -dots[h] / (below * below)
            for level in range(3):
                high = rest.astype(bf16).astype(f32)
                extra = jnp.where(row == level * heads + h, high, extra)
                rest = rest - high
        rows = jnp.concatenate([grad_numer, extra], axis=0)
        first, last = split_images(rows, image, j, middle)
        if first is not None:
            front = add(front, dot_nt(first, feat_query))
        if last is not None:
            back = add(back, dot_nt(last, feat_query))
        gate = jnp.where(pre > 0, spread(states, first, last), 0.0).astype(bf16)
        put(1, j, (dot(omega_back, gate) * scale).astype(bf16))
    parts = []
    for part in (front[:LANES], front[LANES:], back):
        part = jnp.where(mask, part, 0.0)
        total = jnp.sum(part[width:], axis=0, keepdims=True)
        row = lax.broadcasted_iota(jnp.int32, (LANES - width, heads * FEAT), 0)
        parts.append(part[:width])
        parts.append(jnp.where(row == 0, total, 0.0))
    grad_states = jnp.concatenate(parts, axis=0)
    table = jnp.transpose(grad_states).astype(bf16)
    grad_states = grad_states.astype(bf16)
    for j in range(chunks):
        lanes = pl.ds(j * CHUNK, CHUNK)
        image = grid.image[:, j * CHUNK : (j + 1) * CHUNK]
        pre = dot(omega, chunk_of(x_ref, 1, width, j)) * scale
        feat_key = features(pre)
        rows = jnp.concatenate(
            [conv_ref[:, lanes].astype(f32), ones_rows(width, CHUNK, 1)], axis=0
        )
        first, last = split_images(rows, image, j, middle)
        gate = jnp.where(pre > 0, spread(table, first, last), 0.0).astype(bf16)
        put(2, j, (dot(omega_back, gate) * scale).astype(bf16))
        grad_conv_ref[:, lanes] = (
            pick_image(grad_states, feat_key, image, j, middle, width).astype(bf16).astype(f32)
        )
    grad_conv = grad_conv_ref[...]
    values = part_of(x_ref, 2 * width, width).astype(f32)
    taps = taps_ref[...]
    trio = (grid.column_before(values), values, grid.column_after(values))
    moved = (grid.row_below(grad_conv), grad_conv, grid.row_above(grad_conv))
    lane = lax.broadcasted_iota(jnp.int32, (width, LANES), 1)
    small = jnp.where(lane == 9, gain_ref[...], 0.0)
    for r in range(3):
        for c in range(3):
            total = jnp.sum(moved[r] * trio[c], axis=1, keepdims=True)
            small = jnp.where(lane == 3 * r + c, total, small)

    def column_of_taps(c):
        return sum(taps[:, 3 * r + c : 3 * r + c + 1] * moved[r] for r in range(3))

    grad_values = (
        column_of_taps(1)
        + grid.column_after(column_of_taps(0))
        + grid.column_before(column_of_taps(2))
    ).astype(bf16)
    small = jnp.concatenate([small, jnp.zeros((LANES - width, LANES), f32)], axis=0)
    small_ref[...] = jnp.transpose(small)[: small_ref.shape[0]]
    for s in range(x_ref.shape[0]):
        out_ref[s, pl.ds(0, width), :] = normed_ref[s]
        out_ref[s, pl.ds(3 * width, width), :] = grad_values[:, s * LANES : (s + 1) * LANES]


def split_small(small, out_ref, start):
    high = small.astype(bf16)
    out_ref[pl.ds(start, 16), :] = high
    out_ref[pl.ds(start + 16, 16), :] = (small - high.astype(f32)).astype(bf16)


def whole_small(ref, start):
    return ref[pl.ds(start, 16), :].astype(f32) + ref[pl.ds(start + 16, 16), :].astype(f32)


def pack_sum_kernel(parts_ref, small_ref, out_ref):
    packs, rows, _ = parts_ref.shape
    total = jnp.sum(parts_ref[...].astype(f32), axis=0) * (1.0 / packs)
    out_ref[pl.ds(0, rows), :] = total.astype(bf16)
    split_small(small_ref[...] * (1.0 / packs), out_ref, rows)


def join_kernel(own_ref, got_ref, out_ref):
    rows = own_ref.shape[0] - 32
    out_ref[pl.ds(0, rows), :] = own_ref[pl.ds(0, rows), :]
    out_ref[pl.ds(rows, rows), :] = got_ref[pl.ds(0, rows), :]
    split_small(whole_small(own_ref, rows) + whole_small(got_ref, rows), out_ref, 2 * rows)


def unpack_kernel(packs, pack_ref, gathered_ref, weight_ref):
    total = gathered_ref.shape[0] - 32
    rows = total // packs
    width, features_out = weight_ref.shape
    across = features_out // LANES
    for r in range(width // 16):
        for c in range(across):
            block, row = divmod((r * across + c) * 16, rows)
            place = pl.multiple_of((pack_ref[0] ^ block) * rows + row, 16)
            weight_ref[pl.ds(r * 16, 16), pl.ds(c * LANES, LANES)] = gathered_ref[
                pl.ds(place, 16), :
            ].astype(f32)


def spread_kernel(gathered_ref, _, small_ref):
    small = whole_small(gathered_ref, gathered_ref.shape[0] - 32)
    for peer in range(small_ref.shape[0]):
        small_ref[peer] = small


def small_kernel(small_ref, taps_ref, gain_ref):
    groups = small_ref.shape[0]
    width = taps_ref.shape[1] // groups
    for g in range(groups):
        here = pl.ds(g * width, width)
        taps_ref[:, here] = small_ref[g, pl.ds(0, 9), pl.ds(0, width)]
        gain_ref[:, here] = small_ref[g, pl.ds(9, 1), pl.ds(0, width)]


def call(kernel, name, out_shapes, operands, scratch=(), vmem=VMEM, **more):
    return pl.pallas_call(
        kernel,
        name=name,
        out_shape=[jax.ShapeDtypeStruct(shape, kind) for shape, kind in out_shapes],
        scratch_shapes=list(scratch),
        compiler_params=pltpu.CompilerParams(vmem_limit_bytes=vmem),
        **more,
    )(*operands)


def swap(blocks, axis):
    return lax.all_to_all(blocks, axis, split_axis=0, concat_axis=0, tiled=True)


def local(projected, cotangent, out_weight, norm_gain, conv_taps, feature_seeds, packing):
    groups = lax.axis_size("seq")
    member = lax.axis_index("seq")
    packs = lax.axis_size("dp")
    tokens, _, width_all = projected.shape[1:]
    features_out = cotangent.shape[2]
    width = width_all // groups
    heads = width // HEAD
    all_tokens = tokens * groups
    cotangent_all = lax.all_gather(cotangent[0], "seq", axis=0, tiled=True)
    outgoing = call(
        prepare_kernel,
        "prepare",
        [((groups, 3 * width + 16, tokens), bf16)],
        (projected[0].transpose(1, 0, 2), jnp.pad(packing[0], ((0, 11), (0, 0)))),
    )[0]
    seeds = jnp.repeat(lax.dynamic_slice_in_dim(feature_seeds, member * heads, heads, 0), HEAD)
    taps = jnp.pad(
        lax.dynamic_slice_in_dim(conv_taps, member * width, width, 1).T, ((0, 0), (0, 7))
    )
    gain = lax.dynamic_slice_in_dim(norm_gain, member * width, width, 0)[:, None]
    x = swap(outgoing, "seq")
    numer, denom, attention, squares, states, conv, weight_local = call(
        lambda *refs: forward_kernel(heads, *refs),
        "forward",
        [
            ((width, all_tokens), f32),
            ((8, all_tokens), f32),
            ((width, all_tokens), bf16),
            ((groups, groups, LANES), bf16),
            ((3 * LANES, heads * FEAT), bf16),
            ((width, all_tokens), bf16),
            ((width, features_out), bf16),
        ],
        (x, taps, seeds[None], out_weight),
    )
    squares = swap(squares, "seq")
    weight_all = lax.all_gather(weight_local, "seq", axis=0, tiled=True)
    grad_normed, inner = call(
        inner_kernel,
        "inner",
        [((width, all_tokens), f32), ((groups, groups, LANES), bf16)],
        (attention, out_weight, cotangent_all, gain),
        vmem=ALL_VMEM,
        grid=(groups // 8,),
        in_specs=[
            pl.BlockSpec((width, 8 * LANES), lambda i: (0, i)),
            pl.BlockSpec((width, features_out), lambda i: (0, 0)),
            pl.BlockSpec((8 * LANES, features_out), lambda i: (i, 0)),
            pl.BlockSpec((width, 1), lambda i: (0, 0)),
        ],
        out_specs=[
            pl.BlockSpec((width, 8 * LANES), lambda i: (0, i)),
            pl.BlockSpec((groups, groups, LANES), lambda i: (0, 0, 0)),
        ],
        scratch=[pltpu.VMEM((groups, LANES), f32)],
    )
    inner = swap(inner, "seq")
    normed, inverse, weight_tiles, gain_part = call(
        normed_kernel,
        "normed",
        [
            ((groups, width, LANES), bf16),
            ((groups, LANES), f32),
            ((1024, LANES), bf16),
            ((width, LANES), f32),
        ],
        (attention, grad_normed, squares, gain, cotangent_all),
        vmem=ALL_VMEM,
    )
    weight_parts = swap(weight_tiles.reshape(packs, 1024 // packs, LANES), "dp")
    leaving, small = call(
        lambda *refs: backward_kernel(heads, *refs),
        "backward",
        [((groups, 4 * width, LANES), bf16), ((16, LANES), f32)],
        (x, taps, seeds[None], seeds[:, None], numer, denom, states, conv, normed, attention,
         grad_normed, inverse, inner, gain, gain_part),
        vmem=ALL_VMEM,
        scratch=[pltpu.VMEM((width, all_tokens), f32)],
    )
    back = swap(leaving, "seq")
    joined = call(
        pack_sum_kernel,
        "pack_sum",
        [((1024 // packs + 32, LANES), bf16)],
        (weight_parts, small),
    )[0]
    distance = 1
    while distance < packs:
        got = lax.ppermute(joined, "dp", [(i, i ^ distance) for i in range(packs)])
        rows = joined.shape[0] - 32
        joined = call(
            join_kernel, "join", [((2 * rows + 32, LANES), bf16)], (joined, got)
        )[0]
        distance *= 2
    vmem = pl.BlockSpec(memory_space=pltpu.VMEM)
    weight_grad = call(
        lambda *refs: unpack_kernel(packs, *refs),
        "unpack",
        [((width, features_out), f32)],
        (lax.axis_index("dp").astype(jnp.int32)[None], joined),
        in_specs=[pl.BlockSpec(memory_space=pltpu.SMEM), vmem],
    )[0]
    small = call(
        spread_kernel,
        "spread",
        [((groups, 16, LANES), f32)],
        (joined, back),
        in_specs=[vmem, pl.BlockSpec(memory_space=pl.ANY)],
    )[0]
    small = swap(small, "seq")
    across = features_out // 3
    block_out, grads = call(
        finish_kernel,
        "finish",
        [((tokens, features_out), bf16), ((3, tokens, width_all), bf16)],
        (back, back, weight_all),
        vmem=ALL_VMEM,
        grid=(3,),
        in_specs=[
            pl.BlockSpec((groups, width, tokens), lambda i: (0, 0, 0)),
            pl.BlockSpec((groups, width, tokens), lambda i: (0, i + 1, 0)),
            pl.BlockSpec((width_all, across), lambda i: (0, i)),
        ],
        out_specs=[
            pl.BlockSpec((tokens, across), lambda i: (0, i)),
            pl.BlockSpec((1, tokens, width_all), lambda i: (i, 0, 0)),
        ],
        scratch=[pltpu.VMEM((tokens, width_all), bf16)],
    )
    grad_tokens = grads.transpose(1, 0, 2)
    taps_grad, gain_grad = call(
        small_kernel, "small", [((9, width_all), f32), ((1, width_all), f32)], (small,)
    )
    return block_out[None], grad_tokens[None], weight_grad, gain_grad.reshape(-1), taps_grad


def solution(mesh):
    in_specs = (
        P("dp", "seq", None, None),
        P("dp", "seq", None),
        P("seq", None),
        P(),
        P(),
        P(),
        P("dp", None, "seq"),
    )
    out_specs = (P("dp", "seq", None), P("dp", "seq", None, None), P("seq", None), P(), P())
    return jax.shard_map(local, mesh=mesh, in_specs=in_specs, out_specs=out_specs, check_vma=False)
```

```python
import math

import jax
import jax.numpy as jnp
from jax import lax
from jax.experimental import pallas as pl
from jax.experimental.pallas import tpu as pltpu
from jax.sharding import PartitionSpec as P

HEAD = 32
FEAT = 256
LANES = 128
CHUNK = 256
VMEM = 24 * 1024 * 1024
ALL_VMEM = 60 * 1024 * 1024
WIDTHS = (16, 32, 48, 64)

feature_floor = 0.1
epsilon = 1e-06
scale = 1.0 / math.sqrt(HEAD)
bf16, f32 = jnp.bfloat16, jnp.float32


def dot(a, b):
    return lax.dot_general(a, b, (((1,), (0,)), ((), ())), preferred_element_type=f32)


def dot_nt(a, b):
    return lax.dot_general(a, b, (((1,), (1,)), ((), ())), preferred_element_type=f32)


def omega_of(seed, e, f):
    hashed = seed * -1640531535 + (e * FEAT + f)
    hashed = hashed ^ ((hashed >> 16) & 65535)
    hashed = hashed * -2048144789
    hashed = hashed ^ ((hashed >> 13) & 524287)
    hashed = hashed * -1028477387
    hashed = hashed ^ ((hashed >> 16) & 65535)
    uniform = ((hashed >> 8) & 16777215).astype(f32) * (1.0 / 16777216.0)
    return 1.7320508 * (2.0 * uniform - 1.0)


def omega_tall(seed_row, heads):
    shape = (FEAT, heads * HEAD)
    lane = lax.broadcasted_iota(jnp.int32, shape, 1)
    block = omega_of(seed_row, lane % HEAD, lax.broadcasted_iota(jnp.int32, shape, 0))
    return jnp.concatenate(
        [jnp.where(lane // HEAD == h, block, 0.0) for h in range(heads)], axis=0
    ).astype(bf16)


def omega_wide(seed_column, heads):
    shape = (heads * HEAD, FEAT)
    row = lax.broadcasted_iota(jnp.int32, shape, 0)
    block = omega_of(seed_column, row % HEAD, lax.broadcasted_iota(jnp.int32, shape, 1))
    return jnp.concatenate(
        [jnp.where(row // HEAD == h, block, 0.0) for h in range(heads)], axis=1
    ).astype(bf16)


def head_mask(heads):
    shape = (LANES, heads * FEAT)
    row = lax.broadcasted_iota(jnp.int32, shape, 0)
    column = lax.broadcasted_iota(jnp.int32, shape, 1) // FEAT
    width = heads * HEAD
    channel = (row < width) & (row // HEAD == column)
    total = (row >= width) & (row < width + 3 * heads) & ((row - width) % heads == column)
    return channel | total


def chunk_of(ref, part, width, j):
    rows = pl.ds(part * width, width)
    return jnp.concatenate([ref[2 * j, rows, :], ref[2 * j + 1, rows, :]], axis=1)


def part_of(ref, start, count):
    return jnp.concatenate(
        [ref[s, pl.ds(start, count), :] for s in range(ref.shape[0])], axis=1
    )


def by_head(rows, heads):
    return jnp.concatenate(
        [jnp.broadcast_to(rows[h : h + 1], (HEAD, rows.shape[1])) for h in range(heads)], axis=0
    )


def head_sums(values, heads):
    return [
        jnp.sum(values[h * HEAD : (h + 1) * HEAD], axis=0, keepdims=True) for h in range(heads)
    ]


def shifted(values, shift):
    return pltpu.roll(values, shift % values.shape[1], axis=1)


class Grid:
    def __init__(self, ref, start):
        packing = part_of(ref, start, 16).astype(f32)
        self.image, self.row, self.column, self.width, self.height = (
            packing[i : i + 1] for i in range(5)
        )
        self.left = self.column > 0.5
        self.right = self.column < self.width - 1.5
        self.above = self.row > 0.5
        self.below = self.row < self.height - 1.5

    def column_before(self, values):
        return jnp.where(self.left, shifted(values, 1), 0.0)

    def column_after(self, values):
        return jnp.where(self.right, shifted(values, -1), 0.0)

    def by_rows(self, values, inside, sign):
        half = values.shape[1] // 2
        moved = jnp.where(inside & (self.width == 16.0), shifted(values, sign * 16), 0.0)
        front, back = moved[:, :half], moved[:, half:]
        for width in WIDTHS[1:]:
            mask = inside[:, :half] & (self.width[:, :half] == float(width))
            front = front + jnp.where(mask, shifted(values[:, :half], sign * width), 0.0)
        return jnp.concatenate([front, back], axis=1)

    def row_above(self, values):
        return self.by_rows(values, self.above, 1)

    def row_below(self, values):
        return self.by_rows(values, self.below, -1)


def features(pre):
    return (jnp.maximum(pre, 0.0) + feature_floor).astype(bf16)


def split_images(rows, image, j, middle):
    zero = jnp.zeros((), rows.dtype)
    front = back = None
    if j < middle:
        front = jnp.concatenate(
            [jnp.where(image == 0.0, rows, zero), jnp.where(image == 1.0, rows, zero)], axis=0
        ).astype(bf16)
    if j >= middle - 1:
        back = jnp.where(image == 2.0, rows, zero).astype(bf16)
    return front, back


def add(total, term):
    return term if total is None else total + term


def pick_image(left, right, image, j, middle, rows):
    if j < middle - 1:
        both = dot(left[: 2 * LANES], right)
        return jnp.where(image == 0.0, both[:rows], both[LANES : LANES + rows])
    if j >= middle:
        return dot(left[2 * LANES :], right)[:rows]
    every = dot(left, right)
    front = jnp.where(image == 0.0, every[:rows], every[LANES : LANES + rows])
    return jnp.where(image == 2.0, every[2 * LANES : 2 * LANES + rows], front)


def ones_rows(width, columns, count):
    row = lax.broadcasted_iota(jnp.int32, (LANES - width, columns), 0)
    return jnp.where(row < count, 1.0, 0.0)


def prepare_kernel(projected_ref, packing_ref, out_ref):
    groups = out_ref.shape[0]
    width = projected_ref.shape[2] // groups
    turned = jnp.transpose(projected_ref[0])
    here = pl.ds(pl.multiple_of(pl.program_id(0) * width, 16), width)
    for g in range(groups):
        out_ref[g, here, :] = turned[g * width : (g + 1) * width]

    @pl.when(pl.program_id(0) == 0)
    def _():
        rows = packing_ref[...].astype(f32).astype(bf16)
        for g in range(groups):
            out_ref[g, pl.ds(out_ref.shape[1] - 16, 16), :] = rows


def finish_kernel(normed_ref, grad_ref, weight_ref, block_ref, grad_out, turned_ref):
    groups, width, tokens = normed_ref.shape

    @pl.when(pl.program_id(0) == 0)
    def _():
        turned_ref[...] = jnp.transpose(normed_ref[...].reshape(groups * width, tokens))

    grad_out[0] = jnp.transpose(grad_ref[...].reshape(groups * width, tokens))
    block_ref[...] = dot(turned_ref[...], weight_ref[...]).astype(bf16)


def forward_kernel(heads, x_ref, taps_ref, seed_row_ref, weight_ref, _, __,
                   ratio_ref, half_ref, squares_ref, states_ref, weight_out):
    width = heads * HEAD
    chunks = x_ref.shape[0] * LANES // CHUNK
    middle = chunks // 2
    weight_out[...] = weight_ref[...]
    grid = Grid(x_ref, 3 * width)
    values = part_of(x_ref, 2 * width, width).astype(f32)
    taps = taps_ref[...]
    trio = (grid.column_before(values), values, grid.column_after(values))

    def row_of_taps(r):
        return sum(taps[:, 3 * r + c : 3 * r + c + 1] * trio[c] for c in range(3))

    conv = row_of_taps(1) + grid.row_above(row_of_taps(0)) + grid.row_below(row_of_taps(2))
    half_ref[pl.ds(width, width), :] = conv.astype(bf16)
    omega = omega_tall(seed_row_ref[...], heads)
    front = back = None
    for j in range(chunks):
        lanes = pl.ds(j * CHUNK, CHUNK)
        image = grid.image[:, j * CHUNK : (j + 1) * CHUNK]
        rows = jnp.concatenate(
            [half_ref[pl.ds(width, width), lanes].astype(f32), ones_rows(width, CHUNK, 3 * heads)],
            axis=0,
        )
        feat_key = features(dot(omega, chunk_of(x_ref, 1, width, j)) * scale)
        first, last = split_images(rows, image, j, middle)
        if first is not None:
            front = add(front, dot_nt(first, feat_key))
        if last is not None:
            back = add(back, dot_nt(last, feat_key))
    mask = head_mask(heads)
    states = jnp.concatenate(
        [
            jnp.where(mask, part, 0.0).astype(bf16)
            for part in (front[:LANES], front[LANES:], back)
        ],
        axis=0,
    )
    states_ref[...] = states
    squares = []
    for j in range(chunks):
        lanes = pl.ds(j * CHUNK, CHUNK)
        image = grid.image[:, j * CHUNK : (j + 1) * CHUNK]
        feat_query = features(dot(omega, chunk_of(x_ref, 0, width, j)) * scale)
        both = pick_image(states, feat_query, image, j, middle, width + 8)
        ratio_ref[:, lanes] = both
        attention = (both[:width] * by_head(1.0 / both[width:], heads)).astype(bf16)
        half_ref[pl.ds(0, width), lanes] = attention
        attention = attention.astype(f32)
        squares.append(jnp.sum(attention * attention, axis=0, keepdims=True))
    to_peers(squares, squares_ref)


def to_peers(sums, out_ref):
    rows = [
        total[:, part * LANES : (part + 1) * LANES]
        for total in sums
        for part in range(CHUNK // LANES)
    ]
    rows = jnp.concatenate(rows, axis=0).astype(bf16)
    for peer in range(out_ref.shape[0]):
        out_ref[peer] = rows


def tokens_of(values, j):
    return jnp.concatenate([values[2 * j : 2 * j + 1], values[2 * j + 1 : 2 * j + 2]], axis=1)


def inner_kernel(attention_ref, weight_ref, cotangent_ref, gain_ref,
                 grad_normed_ref, inner_ref, rows_ref):
    step = pl.program_id(0)
    chunks = attention_ref.shape[1] // CHUNK
    weight, gain = weight_ref[...], gain_ref[...]
    rows = []
    for j in range(chunks):
        lanes = pl.ds(j * CHUNK, CHUNK)
        grad_normed = dot_nt(weight, cotangent_ref[pl.ds(j * CHUNK, CHUNK), :])
        grad_normed_ref[:, lanes] = grad_normed
        attention = attention_ref[:, lanes].astype(f32)
        inner = jnp.sum(gain * grad_normed * attention, axis=0, keepdims=True)
        for part in range(CHUNK // LANES):
            rows.append(inner[:, part * LANES : (part + 1) * LANES])
    for i, row in enumerate(rows):
        rows_ref[step * len(rows) + i] = row

    @pl.when(step == pl.num_programs(0) - 1)
    def _():
        rows = [rows_ref[i] for i in range(rows_ref.shape[0])]
        rows = jnp.concatenate(rows, axis=0).astype(bf16)
        for peer in range(inner_ref.shape[0]):
            inner_ref[peer] = rows


def normed_kernel(attention_ref, grad_normed_ref, squares_ref, gain_ref, cotangent_ref,
                  normed_ref, inverse_ref, weight_ref, gain_out, rows_ref, total_ref, gain_sum_ref):
    step = pl.program_id(0)
    width, tokens = attention_ref.shape
    chunks = tokens // CHUNK
    groups = squares_ref.shape[0]
    gain = gain_ref[...]

    @pl.when(step == 0)
    def _():
        squares = jnp.sum(squares_ref[...].astype(f32), axis=0)
        inverse = lax.rsqrt(squares * (1.0 / (width * groups)) + epsilon)
        inverse_ref[...] = inverse
        for i in range(groups):
            rows_ref[i] = inverse[i : i + 1]
        total_ref[...] = jnp.zeros_like(total_ref)
        gain_sum_ref[...] = jnp.zeros_like(gain_sum_ref)

    weight, gain_sum = total_ref[...], gain_sum_ref[...]
    for j in range(chunks):
        lanes = pl.ds(j * CHUNK, CHUNK)
        first = (step * chunks + j) * 2
        inv_rms = jnp.concatenate([rows_ref[first], rows_ref[first + 1]], axis=1)
        attention = attention_ref[:, lanes].astype(f32)
        normed = (attention * gain * inv_rms).astype(bf16)
        gain_sum = gain_sum + grad_normed_ref[:, lanes] * attention * inv_rms
        for part in range(CHUNK // LANES):
            normed_ref[2 * j + part] = normed[:, part * LANES : (part + 1) * LANES]
        weight = weight + dot(normed, cotangent_ref[pl.ds(j * CHUNK, CHUNK), :])
    total_ref[...] = weight
    gain_sum_ref[...] = gain_sum

    @pl.when(step == pl.num_programs(0) - 1)
    def _():
        total = jnp.sum(gain_sum_ref[...], axis=1, keepdims=True)
        gain_out[...] = jnp.broadcast_to(total, gain_out.shape)
        across = total_ref.shape[1] // LANES
        for r in range(width // 16):
            for c in range(across):
                weight_ref[pl.ds((r * across + c) * 16, 16), :] = total_ref[
                    pl.ds(r * 16, 16), pl.ds(c * LANES, LANES)
                ].astype(bf16)
        used = width * across
        weight_ref[used:, :] = jnp.zeros((weight_ref.shape[0] - used, LANES), bf16)


def backward_kernel(heads, x_ref, taps_ref, seed_row_ref, seed_column_ref, ratio_ref, half_ref,
                    states_ref, normed_ref, grad_normed_ref,
                    inverse_ref, inner_ref, norm_gain_ref, gain_ref, out_ref, small_ref,
                    grad_conv_ref):
    width = heads * HEAD
    chunks = x_ref.shape[0] * LANES // CHUNK
    middle = chunks // 2
    grid = Grid(x_ref, 3 * width)
    omega = omega_tall(seed_row_ref[...], heads)
    omega_back = omega_wide(seed_column_ref[...], heads)
    states = jnp.transpose(states_ref[...].astype(f32)).astype(bf16)
    mask = head_mask(heads)
    front = back = None
    norm_gain = norm_gain_ref[...]
    inverse = inverse_ref[...]
    away = jnp.sum(inner_ref[...].astype(f32), axis=0) * (1.0 / (width * x_ref.shape[0]))
    away = inverse * inverse * inverse * away

    def put(part, j, values):
        for half in range(CHUNK // LANES):
            out_ref[2 * j + half, pl.ds(part * width, width), :] = values[
                :, half * LANES : (half + 1) * LANES
            ]

    def spread(table, first, last):
        total = None
        if first is not None:
            total = add(total, dot(table[:, : 2 * LANES], first))
        if last is not None:
            total = add(total, dot(table[:, 2 * LANES :], last))
        return total

    for j in range(chunks):
        lanes = pl.ds(j * CHUNK, CHUNK)
        image = grid.image[:, j * CHUNK : (j + 1) * CHUNK]
        pre = dot(omega, chunk_of(x_ref, 0, width, j)) * scale
        feat_query = features(pre)
        grad = tokens_of(inverse, j) * norm_gain * grad_normed_ref[:, lanes]
        grad = grad - half_ref[pl.ds(0, width), lanes].astype(f32) * tokens_of(away, j)
        grad = grad.astype(bf16).astype(f32)
        below = 1.0 / ratio_ref[pl.ds(width, 8), lanes]
        grad_numer = (grad * by_head(below, heads)).astype(bf16).astype(f32)
        dots = head_sums(grad * ratio_ref[pl.ds(0, width), lanes], heads)
        row = lax.broadcasted_iota(jnp.int32, (LANES - width, CHUNK), 0)
        extra = jnp.zeros((LANES - width, CHUNK), f32)
        for h in range(heads):
            rest = -dots[h] * (below[h : h + 1] * below[h : h + 1])
            for level in range(3):
                high = rest.astype(bf16).astype(f32)
                extra = jnp.where(row == level * heads + h, high, extra)
                rest = rest - high
        rows = jnp.concatenate([grad_numer, extra], axis=0)
        first, last = split_images(rows, image, j, middle)
        if first is not None:
            front = add(front, dot_nt(first, feat_query))
        if last is not None:
            back = add(back, dot_nt(last, feat_query))
        gate = jnp.where(pre > 0, spread(states, first, last), 0.0).astype(bf16)
        put(1, j, (dot(omega_back, gate) * scale).astype(bf16))
    parts = []
    for part in (front[:LANES], front[LANES:], back):
        part = jnp.where(mask, part, 0.0)
        total = jnp.sum(part[width:], axis=0, keepdims=True)
        row = lax.broadcasted_iota(jnp.int32, (LANES - width, heads * FEAT), 0)
        parts.append(part[:width])
        parts.append(jnp.where(row == 0, total, 0.0))
    grad_states = jnp.concatenate(parts, axis=0)
    table = jnp.transpose(grad_states).astype(bf16)
    grad_states = grad_states.astype(bf16)
    for j in range(chunks):
        lanes = pl.ds(j * CHUNK, CHUNK)
        image = grid.image[:, j * CHUNK : (j + 1) * CHUNK]
        pre = dot(omega, chunk_of(x_ref, 1, width, j)) * scale
        feat_key = features(pre)
        rows = jnp.concatenate(
            [half_ref[pl.ds(width, width), lanes].astype(f32), ones_rows(width, CHUNK, 1)], axis=0
        )
        first, last = split_images(rows, image, j, middle)
        gate = jnp.where(pre > 0, spread(table, first, last), 0.0).astype(bf16)
        put(2, j, (dot(omega_back, gate) * scale).astype(bf16))
        grad_conv_ref[:, lanes] = (
            pick_image(grad_states, feat_key, image, j, middle, width).astype(bf16).astype(f32)
        )
    grad_conv = grad_conv_ref[...]
    values = part_of(x_ref, 2 * width, width).astype(f32)
    taps = taps_ref[...]
    trio = (grid.column_before(values), values, grid.column_after(values))
    moved = (grid.row_below(grad_conv), grad_conv, grid.row_above(grad_conv))
    lane = lax.broadcasted_iota(jnp.int32, (width, LANES), 1)
    small = jnp.where(lane == 9, gain_ref[...], 0.0)
    for r in range(3):
        for c in range(3):
            total = jnp.sum(moved[r] * trio[c], axis=1, keepdims=True)
            small = jnp.where(lane == 3 * r + c, total, small)

    def column_of_taps(c):
        return sum(taps[:, 3 * r + c : 3 * r + c + 1] * moved[r] for r in range(3))

    grad_values = (
        column_of_taps(1)
        + grid.column_after(column_of_taps(0))
        + grid.column_before(column_of_taps(2))
    ).astype(bf16)
    small = jnp.concatenate([small, jnp.zeros((LANES - width, LANES), f32)], axis=0)
    small_ref[...] = jnp.transpose(small)[: small_ref.shape[0]]
    for s in range(x_ref.shape[0]):
        out_ref[s, pl.ds(0, width), :] = normed_ref[s]
        out_ref[s, pl.ds(3 * width, width), :] = grad_values[:, s * LANES : (s + 1) * LANES]


def split_small(small, out_ref, start):
    high = small.astype(bf16)
    out_ref[pl.ds(start, 16), :] = high
    out_ref[pl.ds(start + 16, 16), :] = (small - high.astype(f32)).astype(bf16)


def whole_small(ref, start):
    return ref[pl.ds(start, 16), :].astype(f32) + ref[pl.ds(start + 16, 16), :].astype(f32)


def pack_sum_kernel(parts_ref, small_ref, out_ref):
    packs, rows, _ = parts_ref.shape
    total = jnp.sum(parts_ref[...].astype(f32), axis=0) * (1.0 / packs)
    out_ref[pl.ds(0, rows), :] = total.astype(bf16)
    split_small(small_ref[...] * (1.0 / packs), out_ref, rows)


def join_kernel(own_ref, got_ref, out_ref):
    rows = own_ref.shape[0] - 32
    out_ref[pl.ds(0, rows), :] = own_ref[pl.ds(0, rows), :]
    out_ref[pl.ds(rows, rows), :] = got_ref[pl.ds(0, rows), :]
    split_small(whole_small(own_ref, rows) + whole_small(got_ref, rows), out_ref, 2 * rows)


def unpack_kernel(packs, pack_ref, gathered_ref, weight_ref):
    total = gathered_ref.shape[0] - 32
    rows = total // packs
    width, features_out = weight_ref.shape
    across = features_out // LANES
    for r in range(width // 16):
        for c in range(across):
            block, row = divmod((r * across + c) * 16, rows)
            place = pl.multiple_of((pack_ref[0] ^ block) * rows + row, 16)
            weight_ref[pl.ds(r * 16, 16), pl.ds(c * LANES, LANES)] = gathered_ref[
                pl.ds(place, 16), :
            ].astype(f32)


def spread_kernel(gathered_ref, _, small_ref):
    small = whole_small(gathered_ref, gathered_ref.shape[0] - 32)
    for peer in range(small_ref.shape[0]):
        small_ref[peer] = small


def small_kernel(small_ref, taps_ref, gain_ref):
    groups = small_ref.shape[0]
    width = taps_ref.shape[1] // groups
    for g in range(groups):
        here = pl.ds(g * width, width)
        taps_ref[:, here] = small_ref[g, pl.ds(0, 9), pl.ds(0, width)]
        gain_ref[:, here] = small_ref[g, pl.ds(9, 1), pl.ds(0, width)]


def call(kernel, name, out_shapes, operands, scratch=(), vmem=VMEM, **more):
    return pl.pallas_call(
        kernel,
        name=name,
        out_shape=[jax.ShapeDtypeStruct(shape, kind) for shape, kind in out_shapes],
        scratch_shapes=list(scratch),
        compiler_params=pltpu.CompilerParams(vmem_limit_bytes=vmem),
        **more,
    )(*operands)


def swap(blocks, axis):
    return lax.all_to_all(blocks, axis, split_axis=0, concat_axis=0, tiled=True)


def local(projected, cotangent, out_weight, norm_gain, conv_taps, feature_seeds, packing):
    groups = lax.axis_size("seq")
    member = lax.axis_index("seq")
    packs = lax.axis_size("dp")
    tokens, _, width_all = projected.shape[1:]
    features_out = cotangent.shape[2]
    width = width_all // groups
    heads = width // HEAD
    all_tokens = tokens * groups
    cotangent_all = lax.all_gather(cotangent[0], "seq", axis=0, tiled=True)
    outgoing = call(
        prepare_kernel,
        "prepare",
        [((groups, 3 * width + 16, tokens), bf16)],
        (projected[0].transpose(1, 0, 2), jnp.pad(packing[0], ((0, 11), (0, 0)))),
        vmem=ALL_VMEM,
        grid=(3,),
        in_specs=[
            pl.BlockSpec((1, tokens, width_all), lambda i: (i, 0, 0)),
            pl.BlockSpec((16, tokens), lambda i: (0, 0)),
        ],
        out_specs=[pl.BlockSpec((groups, 3 * width + 16, tokens), lambda i: (0, 0, 0))],
    )[0]
    seeds = jnp.repeat(lax.dynamic_slice_in_dim(feature_seeds, member * heads, heads, 0), HEAD)
    taps = jnp.pad(
        lax.dynamic_slice_in_dim(conv_taps, member * width, width, 1).T, ((0, 0), (0, 7))
    )
    gain = lax.dynamic_slice_in_dim(norm_gain, member * width, width, 0)[:, None]
    x = swap(outgoing, "seq")
    anywhere = pl.BlockSpec(memory_space=pl.ANY)
    vmem = pl.BlockSpec(memory_space=pltpu.VMEM)
    seed_column = seeds[:, None]
    ratio, half, squares, states, weight_local = call(
        lambda *refs: forward_kernel(heads, *refs),
        "forward",
        [
            ((width + 8, all_tokens), f32),
            ((2 * width, all_tokens), bf16),
            ((groups, groups, LANES), bf16),
            ((3 * LANES, heads * FEAT), bf16),
            ((width, features_out), bf16),
        ],
        (x, taps, seeds[None], out_weight, seed_column, gain),
        in_specs=[vmem, vmem, vmem, vmem, anywhere, anywhere],
    )
    squares = swap(squares, "seq")
    weight_all = lax.all_gather(weight_local, "seq", axis=0, tiled=True)
    steps = groups // 4
    block = 4 * LANES
    grad_normed, inner = call(
        inner_kernel,
        "inner",
        [
            ((width, all_tokens), f32),
            ((groups, groups, LANES), bf16),
        ],
        (half, out_weight, cotangent_all, gain),
        vmem=ALL_VMEM,
        grid=(steps,),
        in_specs=[
            pl.BlockSpec((width, block), lambda i: (0, i)),
            pl.BlockSpec((width, features_out), lambda i: (0, 0)),
            pl.BlockSpec((block, features_out), lambda i: (i, 0)),
            pl.BlockSpec((width, 1), lambda i: (0, 0)),
        ],
        out_specs=[
            pl.BlockSpec((width, block), lambda i: (0, i)),
            pl.BlockSpec((groups, groups, LANES), lambda i: (0, 0, 0)),
        ],
        scratch=[pltpu.VMEM((groups, 1, LANES), f32)],
    )
    inner = swap(inner, "seq")
    normed, inverse, weight_tiles, gain_part = call(
        normed_kernel,
        "normed",
        [
            ((groups, width, LANES), bf16),
            ((groups, LANES), f32),
            ((1024, LANES), bf16),
            ((width, LANES), f32),
        ],
        (half, grad_normed, squares, gain, cotangent_all),
        vmem=ALL_VMEM,
        grid=(steps,),
        in_specs=[
            pl.BlockSpec((width, block), lambda i: (0, i)),
            pl.BlockSpec((width, block), lambda i: (0, i)),
            pl.BlockSpec((groups, groups, LANES), lambda i: (0, 0, 0)),
            pl.BlockSpec((width, 1), lambda i: (0, 0)),
            pl.BlockSpec((block, features_out), lambda i: (i, 0)),
        ],
        out_specs=[
            pl.BlockSpec((groups // steps, width, LANES), lambda i: (i, 0, 0)),
            pl.BlockSpec((groups, LANES), lambda i: (0, 0)),
            pl.BlockSpec((1024, LANES), lambda i: (0, 0)),
            pl.BlockSpec((width, LANES), lambda i: (0, 0)),
        ],
        scratch=[
            pltpu.VMEM((groups, 1, LANES), f32),
            pltpu.VMEM((width, features_out), f32),
            pltpu.VMEM((width, CHUNK), f32),
        ],
    )
    weight_parts = swap(weight_tiles.reshape(packs, 1024 // packs, LANES), "dp")
    leaving, small = call(
        lambda *refs: backward_kernel(heads, *refs),
        "backward",
        [((groups, 4 * width, LANES), bf16), ((16, LANES), f32)],
        (x, taps, seeds[None], seed_column, ratio, half, states, normed,
         grad_normed, inverse, inner, gain, gain_part),
        vmem=ALL_VMEM,
        scratch=[pltpu.VMEM((width, all_tokens), f32)],
    )
    back = swap(leaving, "seq")
    joined = call(
        pack_sum_kernel,
        "pack_sum",
        [((1024 // packs + 32, LANES), bf16)],
        (weight_parts, small),
    )[0]
    distance = 1
    while distance < packs:
        got = lax.ppermute(joined, "dp", [(i, i ^ distance) for i in range(packs)])
        rows = joined.shape[0] - 32
        joined = call(
            join_kernel, "join", [((2 * rows + 32, LANES), bf16)], (joined, got)
        )[0]
        distance *= 2
    weight_grad = call(
        lambda *refs: unpack_kernel(packs, *refs),
        "unpack",
        [((width, features_out), f32)],
        (lax.axis_index("dp").astype(jnp.int32)[None], joined),
        in_specs=[pl.BlockSpec(memory_space=pltpu.SMEM), vmem],
    )[0]
    small = call(
        spread_kernel,
        "spread",
        [((groups, 16, LANES), f32)],
        (joined, back),
        in_specs=[vmem, anywhere],
    )[0]
    small = swap(small, "seq")
    across = features_out // 3
    block_out, grads = call(
        finish_kernel,
        "finish",
        [((tokens, features_out), bf16), ((3, tokens, width_all), bf16)],
        (back, back, weight_all),
        vmem=ALL_VMEM,
        grid=(3,),
        in_specs=[
            pl.BlockSpec((groups, width, tokens), lambda i: (0, 0, 0)),
            pl.BlockSpec((groups, width, tokens), lambda i: (0, i + 1, 0)),
            pl.BlockSpec((width_all, across), lambda i: (0, i)),
        ],
        out_specs=[
            pl.BlockSpec((tokens, across), lambda i: (0, i)),
            pl.BlockSpec((1, tokens, width_all), lambda i: (i, 0, 0)),
        ],
        scratch=[pltpu.VMEM((tokens, width_all), bf16)],
    )
    grad_tokens = grads.transpose(1, 0, 2)
    taps_grad, gain_grad = call(
        small_kernel, "small", [((9, width_all), f32), ((1, width_all), f32)], (small,)
    )
    return block_out[None], grad_tokens[None], weight_grad, gain_grad.reshape(-1), taps_grad


def solution(mesh):
    in_specs = (
        P("dp", "seq", None, None),
        P("dp", "seq", None),
        P("seq", None),
        P(),
        P(),
        P(),
        P("dp", None, "seq"),
    )
    out_specs = (P("dp", "seq", None), P("dp", "seq", None, None), P("seq", None), P(), P())
    return jax.shard_map(local, mesh=mesh, in_specs=in_specs, out_specs=out_specs, check_vma=False)
```

```python
import math

import jax
import jax.numpy as jnp
from jax import lax
from jax.experimental import pallas as pl
from jax.experimental.pallas import tpu as pltpu
from jax.sharding import PartitionSpec as P

HEAD = 32
FEAT = 256
LANES = 128
CHUNK = 256
VMEM = 24 * 1024 * 1024
ALL_VMEM = 60 * 1024 * 1024
WIDTHS = (16, 32, 48, 64)

feature_floor = 0.1
epsilon = 1e-06
scale = 1.0 / math.sqrt(HEAD)
bf16, f32 = jnp.bfloat16, jnp.float32


def dot(a, b):
    return lax.dot_general(a, b, (((1,), (0,)), ((), ())), preferred_element_type=f32)


def dot_nt(a, b):
    return lax.dot_general(a, b, (((1,), (1,)), ((), ())), preferred_element_type=f32)


def omega_of(seed, e, f):
    hashed = seed * -1640531535 + (e * FEAT + f)
    hashed = hashed ^ ((hashed >> 16) & 65535)
    hashed = hashed * -2048144789
    hashed = hashed ^ ((hashed >> 13) & 524287)
    hashed = hashed * -1028477387
    hashed = hashed ^ ((hashed >> 16) & 65535)
    uniform = ((hashed >> 8) & 16777215).astype(f32) * (1.0 / 16777216.0)
    return 1.7320508 * (2.0 * uniform - 1.0)


def omega_tall(seed_row, heads):
    shape = (FEAT, heads * HEAD)
    lane = lax.broadcasted_iota(jnp.int32, shape, 1)
    block = omega_of(seed_row, lane % HEAD, lax.broadcasted_iota(jnp.int32, shape, 0))
    return jnp.concatenate(
        [jnp.where(lane // HEAD == h, block, 0.0) for h in range(heads)], axis=0
    ).astype(bf16)


def omega_wide(seed_column, heads):
    shape = (heads * HEAD, FEAT)
    row = lax.broadcasted_iota(jnp.int32, shape, 0)
    block = omega_of(seed_column, row % HEAD, lax.broadcasted_iota(jnp.int32, shape, 1))
    return jnp.concatenate(
        [jnp.where(row // HEAD == h, block, 0.0) for h in range(heads)], axis=1
    ).astype(bf16)


def head_mask(heads):
    shape = (LANES, heads * FEAT)
    row = lax.broadcasted_iota(jnp.int32, shape, 0)
    column = lax.broadcasted_iota(jnp.int32, shape, 1) // FEAT
    width = heads * HEAD
    channel = (row < width) & (row // HEAD == column)
    total = (row >= width) & (row < width + 3 * heads) & ((row - width) % heads == column)
    return channel | total


def chunk_of(ref, part, width, j):
    rows = pl.ds(part * width, width)
    return jnp.concatenate([ref[2 * j, rows, :], ref[2 * j + 1, rows, :]], axis=1)


def part_of(ref, start, count):
    return jnp.concatenate(
        [ref[s, pl.ds(start, count), :] for s in range(ref.shape[0])], axis=1
    )


def by_head(rows, heads):
    return jnp.concatenate(
        [jnp.broadcast_to(rows[h : h + 1], (HEAD, rows.shape[1])) for h in range(heads)], axis=0
    )


def head_sums(values, heads):
    return [
        jnp.sum(values[h * HEAD : (h + 1) * HEAD], axis=0, keepdims=True) for h in range(heads)
    ]


def shifted(values, shift):
    return pltpu.roll(values, shift % values.shape[1], axis=1)


class Grid:
    def __init__(self, ref, start):
        packing = part_of(ref, start, 16).astype(f32)
        self.image, self.row, self.column, self.width, self.height = (
            packing[i : i + 1] for i in range(5)
        )
        self.left = self.column > 0.5
        self.right = self.column < self.width - 1.5
        self.above = self.row > 0.5
        self.below = self.row < self.height - 1.5

    def column_before(self, values):
        return jnp.where(self.left, shifted(values, 1), 0.0)

    def column_after(self, values):
        return jnp.where(self.right, shifted(values, -1), 0.0)

    def by_rows(self, values, inside, sign):
        half = values.shape[1] // 2
        moved = jnp.where(inside & (self.width == 16.0), shifted(values, sign * 16), 0.0)
        front, back = moved[:, :half], moved[:, half:]
        for width in WIDTHS[1:]:
            mask = inside[:, :half] & (self.width[:, :half] == float(width))
            front = front + jnp.where(mask, shifted(values[:, :half], sign * width), 0.0)
        return jnp.concatenate([front, back], axis=1)

    def row_above(self, values):
        return self.by_rows(values, self.above, 1)

    def row_below(self, values):
        return self.by_rows(values, self.below, -1)


def features(pre):
    return (jnp.maximum(pre, 0.0) + feature_floor).astype(bf16)


def split_images(rows, image, j, middle):
    zero = jnp.zeros((), rows.dtype)
    front = back = None
    if j < middle:
        front = jnp.concatenate(
            [jnp.where(image == 0.0, rows, zero), jnp.where(image == 1.0, rows, zero)], axis=0
        ).astype(bf16)
    if j >= middle - 1:
        back = jnp.where(image == 2.0, rows, zero).astype(bf16)
    return front, back


def add(total, term):
    return term if total is None else total + term


def pick_image(left, right, image, j, middle, rows):
    if j < middle - 1:
        both = dot(left[: 2 * LANES], right)
        return jnp.where(image == 0.0, both[:rows], both[LANES : LANES + rows])
    if j >= middle:
        return dot(left[2 * LANES :], right)[:rows]
    every = dot(left, right)
    front = jnp.where(image == 0.0, every[:rows], every[LANES : LANES + rows])
    return jnp.where(image == 2.0, every[2 * LANES : 2 * LANES + rows], front)


def ones_rows(width, columns, count):
    row = lax.broadcasted_iota(jnp.int32, (LANES - width, columns), 0)
    return jnp.where(row < count, 1.0, 0.0)


def prepare_kernel(projected_ref, packing_ref, out_ref):
    groups = out_ref.shape[0]
    parts, tokens, width_all = projected_ref.shape
    width = width_all // groups
    for part in range(parts):
        turned = jnp.transpose(projected_ref[part])
        for g in range(groups):
            out_ref[g, pl.ds(part * width, width), :] = turned[g * width : (g + 1) * width]
    rows = packing_ref[...].astype(f32).astype(bf16)
    for g in range(groups):
        out_ref[g, pl.ds(parts * width, 16), :] = rows


def finish_kernel(normed_ref, grad_ref, weight_ref, block_ref, grad_out, turned_ref):
    groups, width, tokens = normed_ref.shape

    @pl.when(pl.program_id(0) == 0)
    def _():
        turned_ref[...] = jnp.transpose(normed_ref[...].reshape(groups * width, tokens))

    grad_out[0] = jnp.transpose(grad_ref[...].reshape(groups * width, tokens))
    block_ref[...] = dot(turned_ref[...], weight_ref[...]).astype(bf16)


def forward_kernel(heads, x_ref, taps_ref, seed_row_ref, weight_ref, _, __,
                   ratio_ref, half_ref, squares_ref, states_ref, weight_out):
    width = heads * HEAD
    chunks = x_ref.shape[0] * LANES // CHUNK
    middle = chunks // 2
    weight_out[...] = weight_ref[...]
    grid = Grid(x_ref, 3 * width)
    values = part_of(x_ref, 2 * width, width).astype(f32)
    taps = taps_ref[...]
    trio = (grid.column_before(values), values, grid.column_after(values))

    def row_of_taps(r):
        return sum(taps[:, 3 * r + c : 3 * r + c + 1] * trio[c] for c in range(3))

    conv = row_of_taps(1) + grid.row_above(row_of_taps(0)) + grid.row_below(row_of_taps(2))
    half_ref[pl.ds(width, width), :] = conv.astype(bf16)
    omega = omega_tall(seed_row_ref[...], heads)
    front = back = None
    for j in range(chunks):
        lanes = pl.ds(j * CHUNK, CHUNK)
        image = grid.image[:, j * CHUNK : (j + 1) * CHUNK]
        rows = jnp.concatenate(
            [half_ref[pl.ds(width, width), lanes].astype(f32), ones_rows(width, CHUNK, 3 * heads)],
            axis=0,
        )
        feat_key = features(dot(omega, chunk_of(x_ref, 1, width, j)) * scale)
        first, last = split_images(rows, image, j, middle)
        if first is not None:
            front = add(front, dot_nt(first, feat_key))
        if last is not None:
            back = add(back, dot_nt(last, feat_key))
    mask = head_mask(heads)
    states = jnp.concatenate(
        [
            jnp.where(mask, part, 0.0).astype(bf16)
            for part in (front[:LANES], front[LANES:], back)
        ],
        axis=0,
    )
    states_ref[...] = states
    squares = []
    for j in range(chunks):
        lanes = pl.ds(j * CHUNK, CHUNK)
        image = grid.image[:, j * CHUNK : (j + 1) * CHUNK]
        feat_query = features(dot(omega, chunk_of(x_ref, 0, width, j)) * scale)
        both = pick_image(states, feat_query, image, j, middle, width + 8)
        ratio_ref[:, lanes] = both
        attention = (both[:width] * by_head(1.0 / both[width:], heads)).astype(bf16)
        half_ref[pl.ds(0, width), lanes] = attention
        attention = attention.astype(f32)
        squares.append(jnp.sum(attention * attention, axis=0, keepdims=True))
    to_peers(squares, squares_ref)


def to_peers(sums, out_ref):
    rows = [
        total[:, part * LANES : (part + 1) * LANES]
        for total in sums
        for part in range(CHUNK // LANES)
    ]
    rows = jnp.concatenate(rows, axis=0).astype(bf16)
    for peer in range(out_ref.shape[0]):
        out_ref[peer] = rows


def tokens_of(values, j):
    return jnp.concatenate([values[2 * j : 2 * j + 1], values[2 * j + 1 : 2 * j + 2]], axis=1)


def inner_kernel(attention_ref, weight_ref, cotangent_ref, gain_ref,
                 grad_normed_ref, inner_ref, rows_ref):
    step = pl.program_id(0)
    chunks = attention_ref.shape[1] // CHUNK
    weight, gain = weight_ref[...], gain_ref[...]
    rows = []
    for j in range(chunks):
        lanes = pl.ds(j * CHUNK, CHUNK)
        grad_normed = dot_nt(weight, cotangent_ref[pl.ds(j * CHUNK, CHUNK), :])
        grad_normed_ref[:, lanes] = grad_normed
        attention = attention_ref[:, lanes].astype(f32)
        inner = jnp.sum(gain * grad_normed * attention, axis=0, keepdims=True)
        for part in range(CHUNK // LANES):
            rows.append(inner[:, part * LANES : (part + 1) * LANES])
    for i, row in enumerate(rows):
        rows_ref[step * len(rows) + i] = row

    @pl.when(step == pl.num_programs(0) - 1)
    def _():
        rows = [rows_ref[i] for i in range(rows_ref.shape[0])]
        rows = jnp.concatenate(rows, axis=0).astype(bf16)
        for peer in range(inner_ref.shape[0]):
            inner_ref[peer] = rows


def normed_kernel(attention_ref, grad_normed_ref, squares_ref, gain_ref, cotangent_ref,
                  normed_ref, inverse_ref, weight_ref, gain_out):
    width, tokens = attention_ref.shape
    chunks = tokens // CHUNK
    groups = squares_ref.shape[0]
    gain = gain_ref[...]
    squares = jnp.sum(squares_ref[...].astype(f32), axis=0)
    inverse = lax.rsqrt(squares * (1.0 / (width * groups)) + epsilon)
    inverse_ref[...] = inverse
    weight = gain_sum = None
    for j in range(chunks):
        lanes = pl.ds(j * CHUNK, CHUNK)
        inv_rms = tokens_of(inverse, j)
        attention = attention_ref[:, lanes].astype(f32)
        normed = (attention * gain * inv_rms).astype(bf16)
        gain_sum = add(gain_sum, grad_normed_ref[:, lanes] * attention * inv_rms)
        for part in range(CHUNK // LANES):
            normed_ref[2 * j + part] = normed[:, part * LANES : (part + 1) * LANES]
        weight = add(weight, dot(normed, cotangent_ref[pl.ds(j * CHUNK, CHUNK), :]))
    gain_out[...] = jnp.broadcast_to(jnp.sum(gain_sum, axis=1, keepdims=True), gain_out.shape)
    across = weight.shape[1] // LANES
    weight = weight.astype(bf16)
    for r in range(width // 16):
        for c in range(across):
            weight_ref[pl.ds((r * across + c) * 16, 16), :] = weight[
                r * 16 : (r + 1) * 16, c * LANES : (c + 1) * LANES
            ]
    used = width * across
    weight_ref[used:, :] = jnp.zeros((weight_ref.shape[0] - used, LANES), bf16)


def backward_kernel(heads, x_ref, taps_ref, seed_row_ref, seed_column_ref, ratio_ref, half_ref,
                    states_ref, normed_ref, grad_normed_ref,
                    inverse_ref, inner_ref, norm_gain_ref, gain_ref, out_ref, small_ref,
                    grad_conv_ref):
    width = heads * HEAD
    chunks = x_ref.shape[0] * LANES // CHUNK
    middle = chunks // 2
    grid = Grid(x_ref, 3 * width)
    omega = omega_tall(seed_row_ref[...], heads)
    omega_back = omega_wide(seed_column_ref[...], heads)
    states = jnp.transpose(states_ref[...].astype(f32)).astype(bf16)
    mask = head_mask(heads)
    front = back = None
    norm_gain = norm_gain_ref[...]
    inverse = inverse_ref[...]
    away = jnp.sum(inner_ref[...].astype(f32), axis=0) * (1.0 / (width * x_ref.shape[0]))
    away = inverse * inverse * inverse * away

    def put(part, j, values):
        for half in range(CHUNK // LANES):
            out_ref[2 * j + half, pl.ds(part * width, width), :] = values[
                :, half * LANES : (half + 1) * LANES
            ]

    def spread(table, first, last):
        total = None
        if first is not None:
            total = add(total, dot(table[:, : 2 * LANES], first))
        if last is not None:
            total = add(total, dot(table[:, 2 * LANES :], last))
        return total

    for j in range(chunks):
        lanes = pl.ds(j * CHUNK, CHUNK)
        image = grid.image[:, j * CHUNK : (j + 1) * CHUNK]
        pre = dot(omega, chunk_of(x_ref, 0, width, j)) * scale
        feat_query = features(pre)
        grad = tokens_of(inverse, j) * norm_gain * grad_normed_ref[:, lanes]
        grad = grad - half_ref[pl.ds(0, width), lanes].astype(f32) * tokens_of(away, j)
        grad = grad.astype(bf16).astype(f32)
        below = 1.0 / ratio_ref[pl.ds(width, 8), lanes]
        grad_numer = (grad * by_head(below, heads)).astype(bf16).astype(f32)
        dots = head_sums(grad * ratio_ref[pl.ds(0, width), lanes], heads)
        row = lax.broadcasted_iota(jnp.int32, (LANES - width, CHUNK), 0)
        extra = jnp.zeros((LANES - width, CHUNK), f32)
        for h in range(heads):
            rest = -dots[h] * (below[h : h + 1] * below[h : h + 1])
            for level in range(3):
                high = rest.astype(bf16).astype(f32)
                extra = jnp.where(row == level * heads + h, high, extra)
                rest = rest - high
        rows = jnp.concatenate([grad_numer, extra], axis=0)
        first, last = split_images(rows, image, j, middle)
        if first is not None:
            front = add(front, dot_nt(first, feat_query))
        if last is not None:
            back = add(back, dot_nt(last, feat_query))
        gate = jnp.where(pre > 0, spread(states, first, last), 0.0).astype(bf16)
        put(1, j, (dot(omega_back, gate) * scale).astype(bf16))
    parts = []
    for part in (front[:LANES], front[LANES:], back):
        part = jnp.where(mask, part, 0.0)
        total = jnp.sum(part[width:], axis=0, keepdims=True)
        row = lax.broadcasted_iota(jnp.int32, (LANES - width, heads * FEAT), 0)
        parts.append(part[:width])
        parts.append(jnp.where(row == 0, total, 0.0))
    grad_states = jnp.concatenate(parts, axis=0)
    table = jnp.transpose(grad_states).astype(bf16)
    grad_states = grad_states.astype(bf16)
    for j in range(chunks):
        lanes = pl.ds(j * CHUNK, CHUNK)
        image = grid.image[:, j * CHUNK : (j + 1) * CHUNK]
        pre = dot(omega, chunk_of(x_ref, 1, width, j)) * scale
        feat_key = features(pre)
        rows = jnp.concatenate(
            [half_ref[pl.ds(width, width), lanes].astype(f32), ones_rows(width, CHUNK, 1)], axis=0
        )
        first, last = split_images(rows, image, j, middle)
        gate = jnp.where(pre > 0, spread(table, first, last), 0.0).astype(bf16)
        put(2, j, (dot(omega_back, gate) * scale).astype(bf16))
        grad_conv_ref[:, lanes] = (
            pick_image(grad_states, feat_key, image, j, middle, width).astype(bf16).astype(f32)
        )
    grad_conv = grad_conv_ref[...]
    values = part_of(x_ref, 2 * width, width).astype(f32)
    taps = taps_ref[...]
    trio = (grid.column_before(values), values, grid.column_after(values))
    moved = (grid.row_below(grad_conv), grad_conv, grid.row_above(grad_conv))
    lane = lax.broadcasted_iota(jnp.int32, (width, LANES), 1)
    small = jnp.where(lane == 9, gain_ref[...], 0.0)
    for r in range(3):
        for c in range(3):
            total = jnp.sum(moved[r] * trio[c], axis=1, keepdims=True)
            small = jnp.where(lane == 3 * r + c, total, small)

    def column_of_taps(c):
        return sum(taps[:, 3 * r + c : 3 * r + c + 1] * moved[r] for r in range(3))

    grad_values = (
        column_of_taps(1)
        + grid.column_after(column_of_taps(0))
        + grid.column_before(column_of_taps(2))
    ).astype(bf16)
    small = jnp.concatenate([small, jnp.zeros((LANES - width, LANES), f32)], axis=0)
    small_ref[...] = jnp.transpose(small)[: small_ref.shape[0]]
    for s in range(x_ref.shape[0]):
        out_ref[s, pl.ds(0, width), :] = normed_ref[s]
        out_ref[s, pl.ds(3 * width, width), :] = grad_values[:, s * LANES : (s + 1) * LANES]


def split_small(small, out_ref, start):
    high = small.astype(bf16)
    out_ref[pl.ds(start, 16), :] = high
    out_ref[pl.ds(start + 16, 16), :] = (small - high.astype(f32)).astype(bf16)


def whole_small(ref, start):
    return ref[pl.ds(start, 16), :].astype(f32) + ref[pl.ds(start + 16, 16), :].astype(f32)


def pack_sum_kernel(parts_ref, small_ref, out_ref):
    packs, rows, _ = parts_ref.shape
    total = jnp.sum(parts_ref[...].astype(f32), axis=0) * (1.0 / packs)
    out_ref[pl.ds(0, rows), :] = total.astype(bf16)
    split_small(small_ref[...] * (1.0 / packs), out_ref, rows)


def join_kernel(own_ref, got_ref, out_ref):
    rows = own_ref.shape[0] - 32
    out_ref[pl.ds(0, rows), :] = own_ref[pl.ds(0, rows), :]
    out_ref[pl.ds(rows, rows), :] = got_ref[pl.ds(0, rows), :]
    split_small(whole_small(own_ref, rows) + whole_small(got_ref, rows), out_ref, 2 * rows)


def unpack_kernel(packs, pack_ref, own_ref, got_ref, weight_ref, small_ref, blocks_ref):
    half = own_ref.shape[0] - 32
    rows = 2 * half // packs
    blocks_ref[pl.ds(0, half), :] = own_ref[pl.ds(0, half), :]
    blocks_ref[pl.ds(half, half), :] = got_ref[pl.ds(0, half), :]
    width, features_out = weight_ref.shape
    across = features_out // LANES
    for r in range(width // 16):
        for c in range(across):
            block, row = divmod((r * across + c) * 16, rows)
            place = pl.multiple_of((pack_ref[0] ^ block) * rows + row, 16)
            weight_ref[pl.ds(r * 16, 16), pl.ds(c * LANES, LANES)] = blocks_ref[
                pl.ds(place, 16), :
            ].astype(f32)
    small_ref[...] = whole_small(own_ref, half) + whole_small(got_ref, half)


def spread_kernel(total_ref, _, small_ref):
    small = total_ref[...]
    for peer in range(small_ref.shape[0]):
        small_ref[peer] = small


def small_kernel(small_ref, taps_ref, gain_out, gain_ref):
    groups = small_ref.shape[0]
    width = taps_ref.shape[1] // groups
    for g in range(groups):
        here = pl.ds(g * width, width)
        taps_ref[:, here] = small_ref[g, pl.ds(0, 9), pl.ds(0, width)]
        gain_ref[:, here] = small_ref[g, pl.ds(9, 1), pl.ds(0, width)]
    for r in range(gain_out.shape[0]):
        gain_out[pl.ds(r, 1), :] = gain_ref[:, pl.ds(r * LANES, LANES)]


def call(kernel, name, out_shapes, operands, scratch=(), vmem=VMEM, **more):
    return pl.pallas_call(
        kernel,
        name=name,
        out_shape=[jax.ShapeDtypeStruct(shape, kind) for shape, kind in out_shapes],
        scratch_shapes=list(scratch),
        compiler_params=pltpu.CompilerParams(vmem_limit_bytes=vmem),
        **more,
    )(*operands)


def swap(blocks, axis):
    return lax.all_to_all(blocks, axis, split_axis=0, concat_axis=0, tiled=True)


def local(projected, cotangent, out_weight, norm_gain, conv_taps, feature_seeds, packing):
    groups = lax.axis_size("seq")
    member = lax.axis_index("seq")
    packs = lax.axis_size("dp")
    tokens, _, width_all = projected.shape[1:]
    features_out = cotangent.shape[2]
    width = width_all // groups
    heads = width // HEAD
    all_tokens = tokens * groups
    cotangent_all = lax.all_gather(cotangent[0], "seq", axis=0, tiled=True)
    outgoing = call(
        prepare_kernel,
        "prepare",
        [((groups, 3 * width + 16, tokens), bf16)],
        (projected[0].transpose(1, 0, 2), jnp.pad(packing[0], ((0, 11), (0, 0)))),
    )[0]
    seeds = jnp.repeat(lax.dynamic_slice_in_dim(feature_seeds, member * heads, heads, 0), HEAD)
    taps = jnp.pad(
        lax.dynamic_slice_in_dim(conv_taps, member * width, width, 1).T, ((0, 0), (0, 7))
    )
    gain = lax.dynamic_slice_in_dim(norm_gain, member * width, width, 0)[:, None]
    x = swap(outgoing, "seq")
    anywhere = pl.BlockSpec(memory_space=pl.ANY)
    vmem = pl.BlockSpec(memory_space=pltpu.VMEM)
    seed_column = seeds[:, None]
    ratio, half, squares, states, weight_local = call(
        lambda *refs: forward_kernel(heads, *refs),
        "forward",
        [
            ((width + 8, all_tokens), f32),
            ((2 * width, all_tokens), bf16),
            ((groups, groups, LANES), bf16),
            ((3 * LANES, heads * FEAT), bf16),
            ((width, features_out), bf16),
        ],
        (x, taps, seeds[None], out_weight, seed_column, gain),
        in_specs=[vmem, vmem, vmem, vmem, anywhere, anywhere],
    )
    squares = swap(squares, "seq")
    weight_all = lax.all_gather(weight_local, "seq", axis=0, tiled=True)
    steps = groups // 8
    block = 8 * LANES
    grad_normed, inner = call(
        inner_kernel,
        "inner",
        [
            ((width, all_tokens), f32),
            ((groups, groups, LANES), bf16),
        ],
        (half, out_weight, cotangent_all, gain),
        vmem=ALL_VMEM,
        grid=(steps,),
        in_specs=[
            pl.BlockSpec((width, block), lambda i: (0, i)),
            pl.BlockSpec((width, features_out), lambda i: (0, 0)),
            pl.BlockSpec((block, features_out), lambda i: (i, 0)),
            pl.BlockSpec((width, 1), lambda i: (0, 0)),
        ],
        out_specs=[
            pl.BlockSpec((width, block), lambda i: (0, i)),
            pl.BlockSpec((groups, groups, LANES), lambda i: (0, 0, 0)),
        ],
        scratch=[pltpu.VMEM((groups, 1, LANES), f32)],
    )
    inner = swap(inner, "seq")
    normed, inverse, weight_tiles, gain_part = call(
        normed_kernel,
        "normed",
        [
            ((groups, width, LANES), bf16),
            ((groups, LANES), f32),
            ((1024, LANES), bf16),
            ((width, LANES), f32),
        ],
        (half, grad_normed, squares, gain, cotangent_all),
        vmem=ALL_VMEM,
        grid=(1,),
        in_specs=[
            pl.BlockSpec((width, all_tokens), lambda i: (0, 0)),
            pl.BlockSpec((width, all_tokens), lambda i: (0, 0)),
            pl.BlockSpec((groups, groups, LANES), lambda i: (0, 0, 0)),
            pl.BlockSpec((width, 1), lambda i: (0, 0)),
            pl.BlockSpec((all_tokens, features_out), lambda i: (0, 0)),
        ],
        out_specs=[
            pl.BlockSpec((groups, width, LANES), lambda i: (0, 0, 0)),
            pl.BlockSpec((groups, LANES), lambda i: (0, 0)),
            pl.BlockSpec((1024, LANES), lambda i: (0, 0)),
            pl.BlockSpec((width, LANES), lambda i: (0, 0)),
        ],
    )
    weight_parts = swap(weight_tiles.reshape(packs, 1024 // packs, LANES), "dp")
    leaving, small = call(
        lambda *refs: backward_kernel(heads, *refs),
        "backward",
        [((groups, 4 * width, LANES), bf16), ((16, LANES), f32)],
        (x, taps, seeds[None], seed_column, ratio, half, states, normed,
         grad_normed, inverse, inner, gain, gain_part),
        vmem=ALL_VMEM,
        scratch=[pltpu.VMEM((width, all_tokens), f32)],
    )
    back = swap(leaving, "seq")
    joined = call(
        pack_sum_kernel,
        "pack_sum",
        [((1024 // packs + 32, LANES), bf16)],
        (weight_parts, small),
    )[0]
    distance = 1
    while True:
        got = lax.ppermute(joined, "dp", [(i, i ^ distance) for i in range(packs)])
        distance *= 2
        if distance == packs:
            break
        rows = joined.shape[0] - 32
        joined = call(
            join_kernel, "join", [((2 * rows + 32, LANES), bf16)], (joined, got)
        )[0]
    weight_grad, total = call(
        lambda *refs: unpack_kernel(packs, *refs),
        "unpack",
        [((width, features_out), f32), ((16, LANES), f32)],
        (lax.axis_index("dp").astype(jnp.int32)[None], joined, got),
        in_specs=[pl.BlockSpec(memory_space=pltpu.SMEM), vmem, vmem],
        scratch=[pltpu.VMEM((1024, LANES), bf16)],
    )
    small = call(
        spread_kernel,
        "spread",
        [((groups, 16, LANES), f32)],
        (total, back),
        in_specs=[vmem, anywhere],
    )[0]
    small = swap(small, "seq")
    across = features_out // 3
    block_out, grads = call(
        finish_kernel,
        "finish",
        [((tokens, features_out), bf16), ((3, tokens, width_all), bf16)],
        (back, back, weight_all),
        vmem=ALL_VMEM,
        grid=(3,),
        in_specs=[
            pl.BlockSpec((groups, width, tokens), lambda i: (0, 0, 0)),
            pl.BlockSpec((groups, width, tokens), lambda i: (0, i + 1, 0)),
            pl.BlockSpec((width_all, across), lambda i: (0, i)),
        ],
        out_specs=[
            pl.BlockSpec((tokens, across), lambda i: (0, i)),
            pl.BlockSpec((1, tokens, width_all), lambda i: (i, 0, 0)),
        ],
        scratch=[pltpu.VMEM((tokens, width_all), bf16)],
    )
    grad_tokens = grads.transpose(1, 0, 2)
    taps_grad, gain_grad = call(
        small_kernel,
        "small",
        [((9, width_all), f32), ((width_all // LANES, LANES), f32)],
        (small,),
        scratch=[pltpu.VMEM((1, width_all), f32)],
    )
    return block_out[None], grad_tokens[None], weight_grad, gain_grad.reshape(-1), taps_grad


def solution(mesh):
    in_specs = (
        P("dp", "seq", None, None),
        P("dp", "seq", None),
        P("seq", None),
        P(),
        P(),
        P(),
        P("dp", None, "seq"),
    )
    out_specs = (P("dp", "seq", None), P("dp", "seq", None, None), P("seq", None), P(), P())
    return jax.shard_map(local, mesh=mesh, in_specs=in_specs, out_specs=out_specs, check_vma=False)
```

```python
import math

import jax
import jax.numpy as jnp
from jax import lax
from jax.experimental import pallas as pl
from jax.experimental.pallas import tpu as pltpu
from jax.sharding import PartitionSpec as P

HEAD = 32
FEAT = 256
LANES = 128
CHUNK = 512
PIECES = CHUNK // LANES
VMEM = 24 * 1024 * 1024
ALL_VMEM = 60 * 1024 * 1024
WIDTHS = (16, 32, 48, 64)

feature_floor = 0.1
epsilon = 1e-06
scale = 1.0 / math.sqrt(HEAD)
bf16, f32 = jnp.bfloat16, jnp.float32


def dot(a, b):
    return lax.dot_general(a, b, (((1,), (0,)), ((), ())), preferred_element_type=f32)


def dot_nt(a, b):
    return lax.dot_general(a, b, (((1,), (1,)), ((), ())), preferred_element_type=f32)


def omega_of(seed, e, f):
    hashed = seed * -1640531535 + (e * FEAT + f)
    hashed = hashed ^ ((hashed >> 16) & 65535)
    hashed = hashed * -2048144789
    hashed = hashed ^ ((hashed >> 13) & 524287)
    hashed = hashed * -1028477387
    hashed = hashed ^ ((hashed >> 16) & 65535)
    uniform = ((hashed >> 8) & 16777215).astype(f32) * (1.0 / 16777216.0)
    return 1.7320508 * (2.0 * uniform - 1.0)


def omega_tall(seed_row, heads):
    shape = (FEAT, heads * HEAD)
    lane = lax.broadcasted_iota(jnp.int32, shape, 1)
    block = omega_of(seed_row, lane % HEAD, lax.broadcasted_iota(jnp.int32, shape, 0))
    return jnp.concatenate(
        [jnp.where(lane // HEAD == h, block, 0.0) for h in range(heads)], axis=0
    ).astype(bf16)


def omega_wide(seed_column, heads):
    shape = (heads * HEAD, FEAT)
    row = lax.broadcasted_iota(jnp.int32, shape, 0)
    block = omega_of(seed_column, row % HEAD, lax.broadcasted_iota(jnp.int32, shape, 1))
    return jnp.concatenate(
        [jnp.where(row // HEAD == h, block, 0.0) for h in range(heads)], axis=1
    ).astype(bf16)


def head_mask(heads):
    shape = (LANES, heads * FEAT)
    row = lax.broadcasted_iota(jnp.int32, shape, 0)
    column = lax.broadcasted_iota(jnp.int32, shape, 1) // FEAT
    width = heads * HEAD
    channel = (row < width) & (row // HEAD == column)
    total = (row >= width) & (row < width + 3 * heads) & ((row - width) % heads == column)
    return channel | total


def chunk_of(ref, part, width, j):
    rows = pl.ds(part * width, width)
    return jnp.concatenate([ref[PIECES * j + i, rows, :] for i in range(PIECES)], axis=1)


def part_of(ref, start, count):
    return jnp.concatenate(
        [ref[s, pl.ds(start, count), :] for s in range(ref.shape[0])], axis=1
    )


def by_head(rows, heads):
    return jnp.concatenate(
        [jnp.broadcast_to(rows[h : h + 1], (HEAD, rows.shape[1])) for h in range(heads)], axis=0
    )


def head_sums(values, heads):
    return [
        jnp.sum(values[h * HEAD : (h + 1) * HEAD], axis=0, keepdims=True) for h in range(heads)
    ]


def shifted(values, shift):
    return pltpu.roll(values, shift % values.shape[1], axis=1)


class Grid:
    def __init__(self, ref, start):
        packing = part_of(ref, start, 16).astype(f32)
        self.image, self.row, self.column, self.width, self.height = (
            packing[i : i + 1] for i in range(5)
        )
        self.left = self.column > 0.5
        self.right = self.column < self.width - 1.5
        self.above = self.row > 0.5
        self.below = self.row < self.height - 1.5

    def column_before(self, values):
        return jnp.where(self.left, shifted(values, 1), 0.0)

    def column_after(self, values):
        return jnp.where(self.right, shifted(values, -1), 0.0)

    def by_rows(self, values, inside, sign):
        half = values.shape[1] // 2
        moved = jnp.where(inside & (self.width == 16.0), shifted(values, sign * 16), 0.0)
        front, back = moved[:, :half], moved[:, half:]
        for width in WIDTHS[1:]:
            mask = inside[:, :half] & (self.width[:, :half] == float(width))
            front = front + jnp.where(mask, shifted(values[:, :half], sign * width), 0.0)
        return jnp.concatenate([front, back], axis=1)

    def row_above(self, values):
        return self.by_rows(values, self.above, 1)

    def row_below(self, values):
        return self.by_rows(values, self.below, -1)


def features(pre):
    return (jnp.maximum(pre, 0.0) + feature_floor).astype(bf16)


def split_images(rows, image, j, middle):
    zero = jnp.zeros((), rows.dtype)
    front = back = None
    if j < middle:
        front = jnp.concatenate(
            [jnp.where(image == 0.0, rows, zero), jnp.where(image == 1.0, rows, zero)], axis=0
        ).astype(bf16)
    if j >= middle - 1:
        back = jnp.where(image == 2.0, rows, zero).astype(bf16)
    return front, back


def add(total, term):
    return term if total is None else total + term


def pick_image(left, right, image, j, middle, rows):
    if j < middle - 1:
        both = dot(left[: 2 * LANES], right)
        return jnp.where(image == 0.0, both[:rows], both[LANES : LANES + rows])
    if j >= middle:
        return dot(left[2 * LANES :], right)[:rows]
    every = dot(left, right)
    front = jnp.where(image == 0.0, every[:rows], every[LANES : LANES + rows])
    return jnp.where(image == 2.0, every[2 * LANES : 2 * LANES + rows], front)


def ones_rows(width, columns, count):
    row = lax.broadcasted_iota(jnp.int32, (LANES - width, columns), 0)
    return jnp.where(row < count, 1.0, 0.0)


def prepare_kernel(projected_ref, packing_ref, out_ref):
    groups = out_ref.shape[0]
    parts, tokens, width_all = projected_ref.shape
    width = width_all // groups
    for part in range(parts):
        turned = jnp.transpose(projected_ref[part])
        for g in range(groups):
            out_ref[g, pl.ds(part * width, width), :] = turned[g * width : (g + 1) * width]
    rows = packing_ref[...].astype(f32).astype(bf16)
    for g in range(groups):
        out_ref[g, pl.ds(parts * width, 16), :] = rows


def finish_kernel(normed_ref, grad_ref, weight_ref, block_ref, grad_out, turned_ref):
    groups, width, tokens = normed_ref.shape

    @pl.when(pl.program_id(0) == 0)
    def _():
        turned_ref[...] = jnp.transpose(normed_ref[...].reshape(groups * width, tokens))

    grad_out[0] = jnp.transpose(grad_ref[...].reshape(groups * width, tokens))
    block_ref[...] = dot(turned_ref[...], weight_ref[...]).astype(bf16)


def forward_kernel(heads, x_ref, taps_ref, seed_row_ref, weight_ref, _, __,
                   ratio_ref, half_ref, squares_ref, states_ref, weight_out):
    width = heads * HEAD
    chunks = x_ref.shape[0] * LANES // CHUNK
    middle = chunks // 2
    weight_out[...] = weight_ref[...]
    grid = Grid(x_ref, 3 * width)
    values = part_of(x_ref, 2 * width, width).astype(f32)
    taps = taps_ref[...]
    trio = (grid.column_before(values), values, grid.column_after(values))

    def row_of_taps(r):
        return sum(taps[:, 3 * r + c : 3 * r + c + 1] * trio[c] for c in range(3))

    conv = row_of_taps(1) + grid.row_above(row_of_taps(0)) + grid.row_below(row_of_taps(2))
    half_ref[pl.ds(width, width), :] = conv.astype(bf16)
    omega = omega_tall(seed_row_ref[...], heads)
    front = back = None
    for j in range(chunks):
        lanes = pl.ds(j * CHUNK, CHUNK)
        image = grid.image[:, j * CHUNK : (j + 1) * CHUNK]
        rows = jnp.concatenate(
            [half_ref[pl.ds(width, width), lanes].astype(f32), ones_rows(width, CHUNK, 3 * heads)],
            axis=0,
        )
        feat_key = features(dot(omega, chunk_of(x_ref, 1, width, j)) * scale)
        first, last = split_images(rows, image, j, middle)
        if first is not None:
            front = add(front, dot_nt(first, feat_key))
        if last is not None:
            back = add(back, dot_nt(last, feat_key))
    mask = head_mask(heads)
    states = jnp.concatenate(
        [
            jnp.where(mask, part, 0.0).astype(bf16)
            for part in (front[:LANES], front[LANES:], back)
        ],
        axis=0,
    )
    states_ref[...] = states
    squares = []
    for j in range(chunks):
        lanes = pl.ds(j * CHUNK, CHUNK)
        image = grid.image[:, j * CHUNK : (j + 1) * CHUNK]
        feat_query = features(dot(omega, chunk_of(x_ref, 0, width, j)) * scale)
        both = pick_image(states, feat_query, image, j, middle, width + 8)
        ratio_ref[:, lanes] = both
        attention = (both[:width] * by_head(1.0 / both[width:], heads)).astype(bf16)
        half_ref[pl.ds(0, width), lanes] = attention
        attention = attention.astype(f32)
        squares.append(jnp.sum(attention * attention, axis=0, keepdims=True))
    to_peers(squares, squares_ref)


def to_peers(sums, out_ref):
    rows = [
        total[:, part * LANES : (part + 1) * LANES]
        for total in sums
        for part in range(PIECES)
    ]
    rows = jnp.concatenate(rows, axis=0).astype(bf16)
    for peer in range(out_ref.shape[0]):
        out_ref[peer] = rows


def tokens_of(values, j):
    first = PIECES * j
    return jnp.concatenate([values[first + i : first + i + 1] for i in range(PIECES)], axis=1)


def inner_kernel(attention_ref, weight_ref, cotangent_ref, gain_ref,
                 grad_normed_ref, inner_ref, rows_ref):
    step = pl.program_id(0)
    chunks = attention_ref.shape[1] // CHUNK
    weight, gain = weight_ref[...], gain_ref[...]
    rows = []
    for j in range(chunks):
        lanes = pl.ds(j * CHUNK, CHUNK)
        grad_normed = dot_nt(weight, cotangent_ref[pl.ds(j * CHUNK, CHUNK), :])
        grad_normed_ref[:, lanes] = grad_normed
        attention = attention_ref[:, lanes].astype(f32)
        inner = jnp.sum(gain * grad_normed * attention, axis=0, keepdims=True)
        for part in range(PIECES):
            rows.append(inner[:, part * LANES : (part + 1) * LANES])
    for i, row in enumerate(rows):
        rows_ref[step * len(rows) + i] = row

    @pl.when(step == pl.num_programs(0) - 1)
    def _():
        rows = [rows_ref[i] for i in range(rows_ref.shape[0])]
        rows = jnp.concatenate(rows, axis=0).astype(bf16)
        for peer in range(inner_ref.shape[0]):
            inner_ref[peer] = rows


def normed_kernel(attention_ref, grad_normed_ref, squares_ref, gain_ref, cotangent_ref,
                  normed_ref, inverse_ref, weight_ref, gain_out):
    width, tokens = attention_ref.shape
    chunks = tokens // CHUNK
    groups = squares_ref.shape[0]
    gain = gain_ref[...]
    squares = jnp.sum(squares_ref[...].astype(f32), axis=0)
    inverse = lax.rsqrt(squares * (1.0 / (width * groups)) + epsilon)
    inverse_ref[...] = inverse
    weight = gain_sum = None
    for j in range(chunks):
        lanes = pl.ds(j * CHUNK, CHUNK)
        inv_rms = tokens_of(inverse, j)
        attention = attention_ref[:, lanes].astype(f32)
        normed = (attention * gain * inv_rms).astype(bf16)
        gain_sum = add(gain_sum, grad_normed_ref[:, lanes] * attention * inv_rms)
        for part in range(PIECES):
            normed_ref[PIECES * j + part] = normed[:, part * LANES : (part + 1) * LANES]
        weight = add(weight, dot(normed, cotangent_ref[pl.ds(j * CHUNK, CHUNK), :]))
    gain_out[...] = jnp.broadcast_to(jnp.sum(gain_sum, axis=1, keepdims=True), gain_out.shape)
    across = weight.shape[1] // LANES
    weight = weight.astype(bf16)
    for r in range(width // 16):
        for c in range(across):
            weight_ref[pl.ds((r * across + c) * 16, 16), :] = weight[
                r * 16 : (r + 1) * 16, c * LANES : (c + 1) * LANES
            ]
    used = width * across
    weight_ref[used:, :] = jnp.zeros((weight_ref.shape[0] - used, LANES), bf16)


def backward_kernel(heads, x_ref, taps_ref, seed_row_ref, seed_column_ref, ratio_ref, half_ref,
                    states_ref, normed_ref, grad_normed_ref,
                    inverse_ref, inner_ref, norm_gain_ref, gain_ref, out_ref, small_ref,
                    grad_conv_ref):
    width = heads * HEAD
    chunks = x_ref.shape[0] * LANES // CHUNK
    middle = chunks // 2
    grid = Grid(x_ref, 3 * width)
    omega = omega_tall(seed_row_ref[...], heads)
    omega_back = omega_wide(seed_column_ref[...], heads)
    states = jnp.transpose(states_ref[...].astype(f32)).astype(bf16)
    mask = head_mask(heads)
    front = back = None
    norm_gain = norm_gain_ref[...]
    inverse = inverse_ref[...]
    away = jnp.sum(inner_ref[...].astype(f32), axis=0) * (1.0 / (width * x_ref.shape[0]))
    away = inverse * inverse * inverse * away

    def put(part, j, values):
        for half in range(PIECES):
            out_ref[PIECES * j + half, pl.ds(part * width, width), :] = values[
                :, half * LANES : (half + 1) * LANES
            ]

    def spread(table, first, last):
        total = None
        if first is not None:
            total = add(total, dot(table[:, : 2 * LANES], first))
        if last is not None:
            total = add(total, dot(table[:, 2 * LANES :], last))
        return total

    for j in range(chunks):
        lanes = pl.ds(j * CHUNK, CHUNK)
        image = grid.image[:, j * CHUNK : (j + 1) * CHUNK]
        pre = dot(omega, chunk_of(x_ref, 0, width, j)) * scale
        feat_query = features(pre)
        grad = tokens_of(inverse, j) * norm_gain * grad_normed_ref[:, lanes]
        grad = grad - half_ref[pl.ds(0, width), lanes].astype(f32) * tokens_of(away, j)
        grad = grad.astype(bf16).astype(f32)
        below = 1.0 / ratio_ref[pl.ds(width, 8), lanes]
        grad_numer = (grad * by_head(below, heads)).astype(bf16).astype(f32)
        dots = head_sums(grad * ratio_ref[pl.ds(0, width), lanes], heads)
        row = lax.broadcasted_iota(jnp.int32, (LANES - width, CHUNK), 0)
        extra = jnp.zeros((LANES - width, CHUNK), f32)
        for h in range(heads):
            rest = -dots[h] * (below[h : h + 1] * below[h : h + 1])
            for level in range(3):
                high = rest.astype(bf16).astype(f32)
                extra = jnp.where(row == level * heads + h, high, extra)
                rest = rest - high
        rows = jnp.concatenate([grad_numer, extra], axis=0)
        first, last = split_images(rows, image, j, middle)
        if first is not None:
            front = add(front, dot_nt(first, feat_query))
        if last is not None:
            back = add(back, dot_nt(last, feat_query))
        gate = jnp.where(pre > 0, spread(states, first, last), 0.0).astype(bf16)
        put(1, j, (dot(omega_back, gate) * scale).astype(bf16))
    parts = []
    for part in (front[:LANES], front[LANES:], back):
        part = jnp.where(mask, part, 0.0)
        total = jnp.sum(part[width:], axis=0, keepdims=True)
        row = lax.broadcasted_iota(jnp.int32, (LANES - width, heads * FEAT), 0)
        parts.append(part[:width])
        parts.append(jnp.where(row == 0, total, 0.0))
    grad_states = jnp.concatenate(parts, axis=0)
    table = jnp.transpose(grad_states).astype(bf16)
    grad_states = grad_states.astype(bf16)
    for j in range(chunks):
        lanes = pl.ds(j * CHUNK, CHUNK)
        image = grid.image[:, j * CHUNK : (j + 1) * CHUNK]
        pre = dot(omega, chunk_of(x_ref, 1, width, j)) * scale
        feat_key = features(pre)
        rows = jnp.concatenate(
            [half_ref[pl.ds(width, width), lanes].astype(f32), ones_rows(width, CHUNK, 1)], axis=0
        )
        first, last = split_images(rows, image, j, middle)
        gate = jnp.where(pre > 0, spread(table, first, last), 0.0).astype(bf16)
        put(2, j, (dot(omega_back, gate) * scale).astype(bf16))
        grad_conv_ref[:, lanes] = (
            pick_image(grad_states, feat_key, image, j, middle, width).astype(bf16).astype(f32)
        )
    grad_conv = grad_conv_ref[...]
    values = part_of(x_ref, 2 * width, width).astype(f32)
    taps = taps_ref[...]
    trio = (grid.column_before(values), values, grid.column_after(values))
    moved = (grid.row_below(grad_conv), grad_conv, grid.row_above(grad_conv))
    lane = lax.broadcasted_iota(jnp.int32, (width, LANES), 1)
    small = jnp.where(lane == 9, gain_ref[...], 0.0)
    for r in range(3):
        for c in range(3):
            total = jnp.sum(moved[r] * trio[c], axis=1, keepdims=True)
            small = jnp.where(lane == 3 * r + c, total, small)

    def column_of_taps(c):
        return sum(taps[:, 3 * r + c : 3 * r + c + 1] * moved[r] for r in range(3))

    grad_values = (
        column_of_taps(1)
        + grid.column_after(column_of_taps(0))
        + grid.column_before(column_of_taps(2))
    ).astype(bf16)
    small = jnp.concatenate([small, jnp.zeros((LANES - width, LANES), f32)], axis=0)
    small_ref[...] = jnp.transpose(small)[: small_ref.shape[0]]
    for s in range(x_ref.shape[0]):
        out_ref[s, pl.ds(0, width), :] = normed_ref[s]
        out_ref[s, pl.ds(3 * width, width), :] = grad_values[:, s * LANES : (s + 1) * LANES]


def split_small(small, out_ref, start):
    high = small.astype(bf16)
    out_ref[pl.ds(start, 16), :] = high
    out_ref[pl.ds(start + 16, 16), :] = (small - high.astype(f32)).astype(bf16)


def whole_small(ref, start):
    return ref[pl.ds(start, 16), :].astype(f32) + ref[pl.ds(start + 16, 16), :].astype(f32)


def pack_sum_kernel(parts_ref, small_ref, out_ref):
    packs, rows, _ = parts_ref.shape
    total = jnp.sum(parts_ref[...].astype(f32), axis=0) * (1.0 / packs)
    out_ref[pl.ds(0, rows), :] = total.astype(bf16)
    split_small(small_ref[...] * (1.0 / packs), out_ref, rows)


def join_kernel(own_ref, got_ref, out_ref):
    rows = own_ref.shape[0] - 32
    out_ref[pl.ds(0, rows), :] = own_ref[pl.ds(0, rows), :]
    out_ref[pl.ds(rows, rows), :] = got_ref[pl.ds(0, rows), :]
    split_small(whole_small(own_ref, rows) + whole_small(got_ref, rows), out_ref, 2 * rows)


def unpack_kernel(packs, pack_ref, own_ref, got_ref, weight_ref, small_ref, blocks_ref):
    half = own_ref.shape[0] - 32
    rows = 2 * half // packs
    blocks_ref[pl.ds(0, half), :] = own_ref[pl.ds(0, half), :]
    blocks_ref[pl.ds(half, half), :] = got_ref[pl.ds(0, half), :]
    width, features_out = weight_ref.shape
    across = features_out // LANES
    for r in range(width // 16):
        for c in range(across):
            block, row = divmod((r * across + c) * 16, rows)
            place = pl.multiple_of((pack_ref[0] ^ block) * rows + row, 16)
            weight_ref[pl.ds(r * 16, 16), pl.ds(c * LANES, LANES)] = blocks_ref[
                pl.ds(place, 16), :
            ].astype(f32)
    small_ref[...] = whole_small(own_ref, half) + whole_small(got_ref, half)


def spread_kernel(total_ref, _, small_ref):
    small = total_ref[...]
    for peer in range(small_ref.shape[0]):
        small_ref[peer] = small


def small_kernel(small_ref, taps_ref, gain_out, gain_ref):
    groups = small_ref.shape[0]
    width = taps_ref.shape[1] // groups
    for g in range(groups):
        here = pl.ds(g * width, width)
        taps_ref[:, here] = small_ref[g, pl.ds(0, 9), pl.ds(0, width)]
        gain_ref[:, here] = small_ref[g, pl.ds(9, 1), pl.ds(0, width)]
    for r in range(gain_out.shape[0]):
        gain_out[pl.ds(r, 1), :] = gain_ref[:, pl.ds(r * LANES, LANES)]


def call(kernel, name, out_shapes, operands, scratch=(), vmem=VMEM, **more):
    return pl.pallas_call(
        kernel,
        name=name,
        out_shape=[jax.ShapeDtypeStruct(shape, kind) for shape, kind in out_shapes],
        scratch_shapes=list(scratch),
        compiler_params=pltpu.CompilerParams(vmem_limit_bytes=vmem),
        **more,
    )(*operands)


def swap(blocks, axis):
    return lax.all_to_all(blocks, axis, split_axis=0, concat_axis=0, tiled=True)


def local(projected, cotangent, out_weight, norm_gain, conv_taps, feature_seeds, packing):
    groups = lax.axis_size("seq")
    member = lax.axis_index("seq")
    packs = lax.axis_size("dp")
    tokens, _, width_all = projected.shape[1:]
    features_out = cotangent.shape[2]
    width = width_all // groups
    heads = width // HEAD
    all_tokens = tokens * groups
    cotangent_all = lax.all_gather(cotangent[0], "seq", axis=0, tiled=True)
    outgoing = call(
        prepare_kernel,
        "prepare",
        [((groups, 3 * width + 16, tokens), bf16)],
        (projected[0].transpose(1, 0, 2), jnp.pad(packing[0], ((0, 11), (0, 0)))),
    )[0]
    seeds = jnp.repeat(lax.dynamic_slice_in_dim(feature_seeds, member * heads, heads, 0), HEAD)
    taps = jnp.pad(
        lax.dynamic_slice_in_dim(conv_taps, member * width, width, 1).T, ((0, 0), (0, 7))
    )
    gain = lax.dynamic_slice_in_dim(norm_gain, member * width, width, 0)[:, None]
    x = swap(outgoing, "seq")
    anywhere = pl.BlockSpec(memory_space=pl.ANY)
    vmem = pl.BlockSpec(memory_space=pltpu.VMEM)
    seed_column = seeds[:, None]
    ratio, half, squares, states, weight_local = call(
        lambda *refs: forward_kernel(heads, *refs),
        "forward",
        [
            ((width + 8, all_tokens), f32),
            ((2 * width, all_tokens), bf16),
            ((groups, groups, LANES), bf16),
            ((3 * LANES, heads * FEAT), bf16),
            ((width, features_out), bf16),
        ],
        (x, taps, seeds[None], out_weight, seed_column, gain),
        in_specs=[vmem, vmem, vmem, vmem, anywhere, anywhere],
    )
    squares = swap(squares, "seq")
    weight_all = lax.all_gather(weight_local, "seq", axis=0, tiled=True)
    steps = groups // 8
    block = 8 * LANES
    grad_normed, inner = call(
        inner_kernel,
        "inner",
        [
            ((width, all_tokens), f32),
            ((groups, groups, LANES), bf16),
        ],
        (half, out_weight, cotangent_all, gain),
        vmem=ALL_VMEM,
        grid=(steps,),
        in_specs=[
            pl.BlockSpec((width, block), lambda i: (0, i)),
            pl.BlockSpec((width, features_out), lambda i: (0, 0)),
            pl.BlockSpec((block, features_out), lambda i: (i, 0)),
            pl.BlockSpec((width, 1), lambda i: (0, 0)),
        ],
        out_specs=[
            pl.BlockSpec((width, block), lambda i: (0, i)),
            pl.BlockSpec((groups, groups, LANES), lambda i: (0, 0, 0)),
        ],
        scratch=[pltpu.VMEM((groups, 1, LANES), f32)],
    )
    inner = swap(inner, "seq")
    normed, inverse, weight_tiles, gain_part = call(
        normed_kernel,
        "normed",
        [
            ((groups, width, LANES), bf16),
            ((groups, LANES), f32),
            ((1024, LANES), bf16),
            ((width, LANES), f32),
        ],
        (half, grad_normed, squares, gain, cotangent_all),
        vmem=ALL_VMEM,
        grid=(1,),
        in_specs=[
            pl.BlockSpec((width, all_tokens), lambda i: (0, 0)),
            pl.BlockSpec((width, all_tokens), lambda i: (0, 0)),
            pl.BlockSpec((groups, groups, LANES), lambda i: (0, 0, 0)),
            pl.BlockSpec((width, 1), lambda i: (0, 0)),
            pl.BlockSpec((all_tokens, features_out), lambda i: (0, 0)),
        ],
        out_specs=[
            pl.BlockSpec((groups, width, LANES), lambda i: (0, 0, 0)),
            pl.BlockSpec((groups, LANES), lambda i: (0, 0)),
            pl.BlockSpec((1024, LANES), lambda i: (0, 0)),
            pl.BlockSpec((width, LANES), lambda i: (0, 0)),
        ],
    )
    weight_parts = swap(weight_tiles.reshape(packs, 1024 // packs, LANES), "dp")
    leaving, small = call(
        lambda *refs: backward_kernel(heads, *refs),
        "backward",
        [((groups, 4 * width, LANES), bf16), ((16, LANES), f32)],
        (x, taps, seeds[None], seed_column, ratio, half, states, normed,
         grad_normed, inverse, inner, gain, gain_part),
        vmem=ALL_VMEM,
        scratch=[pltpu.VMEM((width, all_tokens), f32)],
    )
    back = swap(leaving, "seq")
    joined = call(
        pack_sum_kernel,
        "pack_sum",
        [((1024 // packs + 32, LANES), bf16)],
        (weight_parts, small),
    )[0]
    distance = 1
    while True:
        got = lax.ppermute(joined, "dp", [(i, i ^ distance) for i in range(packs)])
        distance *= 2
        if distance == packs:
            break
        rows = joined.shape[0] - 32
        joined = call(
            join_kernel, "join", [((2 * rows + 32, LANES), bf16)], (joined, got)
        )[0]
    weight_grad, total = call(
        lambda *refs: unpack_kernel(packs, *refs),
        "unpack",
        [((width, features_out), f32), ((16, LANES), f32)],
        (lax.axis_index("dp").astype(jnp.int32)[None], joined, got),
        in_specs=[pl.BlockSpec(memory_space=pltpu.SMEM), vmem, vmem],
        scratch=[pltpu.VMEM((1024, LANES), bf16)],
    )
    small = call(
        spread_kernel,
        "spread",
        [((groups, 16, LANES), f32)],
        (total, back),
        in_specs=[vmem, anywhere],
    )[0]
    small = swap(small, "seq")
    across = features_out // 3
    block_out, grads = call(
        finish_kernel,
        "finish",
        [((tokens, features_out), bf16), ((3, tokens, width_all), bf16)],
        (back, back, weight_all),
        vmem=ALL_VMEM,
        grid=(3,),
        in_specs=[
            pl.BlockSpec((groups, width, tokens), lambda i: (0, 0, 0)),
            pl.BlockSpec((groups, width, tokens), lambda i: (0, i + 1, 0)),
            pl.BlockSpec((width_all, across), lambda i: (0, i)),
        ],
        out_specs=[
            pl.BlockSpec((tokens, across), lambda i: (0, i)),
            pl.BlockSpec((1, tokens, width_all), lambda i: (i, 0, 0)),
        ],
        scratch=[pltpu.VMEM((tokens, width_all), bf16)],
    )
    grad_tokens = grads.transpose(1, 0, 2)
    taps_grad, gain_grad = call(
        small_kernel,
        "small",
        [((9, width_all), f32), ((width_all // LANES, LANES), f32)],
        (small,),
        scratch=[pltpu.VMEM((1, width_all), f32)],
    )
    return block_out[None], grad_tokens[None], weight_grad, gain_grad.reshape(-1), taps_grad


def solution(mesh):
    in_specs = (
        P("dp", "seq", None, None),
        P("dp", "seq", None),
        P("seq", None),
        P(),
        P(),
        P(),
        P("dp", None, "seq"),
    )
    out_specs = (P("dp", "seq", None), P("dp", "seq", None, None), P("seq", None), P(), P())
    return jax.shard_map(local, mesh=mesh, in_specs=in_specs, out_specs=out_specs, check_vma=False)
```
